32 devices in a mesh: seq: 2 (over core), dp: 16 (over z, y, x).
Axes of the slice: x: 2, y: 2, z: 4, core: 2. Of those that a mesh axis runs over, the one named last changes fastest.
Arguments:
- hidden: bfloat16 [16, 512, 2560], P('dp', 'seq'), may hold values from -6 to 6
- scan_input: bfloat16 [16, 512, 2560], P('dp', 'seq'), may hold values from -6 to 6
- grad_out: bfloat16 [16, 512, 2560], P('dp', 'seq'), may hold values from -6 to 6
- step_size: float32 [16, 40, 512], P('dp', None, 'seq'), may hold values from 0.5 to 400
- proj_weight: bfloat16 [2560, 256], replicated, may hold values from -0.0068359375 to 0.0068359375
- log_rate: float32 [40], replicated, may hold values from -7.825 to -3.506
- skip_gain: float32 [40], replicated, may hold values from 0.5 to 1.5
- tile_list: int32 [16, 2], P('dp', 'seq'), may hold values from 0 to 1, as said below
Outputs:
- grad_input: bfloat16 [16, 512, 2560], P('dp', 'seq')
- grad_step: float32 [16, 40, 512], P('dp', None, 'seq')
- grad_weight: float32 [2560, 256], P('seq')
- grad_rate: float32 [40], P('seq')
- grad_skip: float32 [40], P('seq')
The draws below stay inside these ranges and needn't reach their ends.
Inputs may be any that keep to these rules, and one draw needn't show every extreme that they name: `tile_list`: for each device, its 1 entries list the local indices of its valid groups in increasing order, then 1 in every unused entry; in every draw some device has the one group valid.
All inputs are finite; a program needn't handle non-finite values.
Results may differ from the reference program's by a relative error of at most 0.003.
Values sent between devices are 32-bit elements; how exact they have to be, the bound alone decides.
A program may use at most 192 MiB of HBM per device.

```python
import math
import jax
import jax.numpy as jnp
from jax import lax

D = 2560
HEADS = 40
HEAD_DIM = 64
STATE = 128
GROUP = 256
CH_DEV = 1
LEN = 512
GROUPS = 2
SCENES = 16
DI = 2560
N_SEQ = 2


def draw_step_size(key, part):
    key = jax.random.fold_in(key, 11)
    first, second = jax.random.split(key)
    shape = (SCENES, HEADS, LEN)
    base = jnp.exp(jax.random.uniform(first, shape, jnp.float32, math.log(0.5), math.log(2.0)))
    spots = jax.random.randint(second, (SCENES, 2), 0, LEN)
    where_ids = jnp.arange(LEN, dtype=jnp.int32)
    struck = jnp.any(where_ids[None, None, :] == spots[:, :, None], axis=1)
    return jnp.where(struck[:, None, :], 400.0, base).astype(jnp.float32)


def draw_log_rate(key, part):
    key = jax.random.fold_in(key, 23)
    upper_end = math.log(0.03)
    return jax.random.uniform(key, (HEADS,), jnp.float32, math.log(0.0004), upper_end)


def draw_tile_list(key, part):
    key = jax.random.fold_in(key, 37)
    first, second, third = jax.random.split(key, 3)
    valid_bits = jax.random.randint(first, (SCENES, N_SEQ, CH_DEV), 0, 5) < 3
    full_scene = jax.random.randint(second, (), 0, SCENES)
    full_shard = jax.random.randint(third, (), 0, N_SEQ)
    scene_ids = jnp.arange(SCENES, dtype=jnp.int32)[:, None, None]
    shard_ids = jnp.arange(N_SEQ, dtype=jnp.int32)[None, :, None]
    valid_bits = valid_bits | (scene_ids == full_scene) & (shard_ids == full_shard)
    slot_ids = jnp.arange(CH_DEV, dtype=jnp.int32)[None, None, :]
    ranked = jnp.sort(jnp.where(valid_bits, slot_ids, CH_DEV + slot_ids), axis=2)
    listed = jnp.where(ranked < CH_DEV, ranked, CH_DEV)
    return listed.reshape(SCENES, GROUPS).astype(jnp.int32)


def level_of(rng, shape, cuts, smallest, top_value):
    def one(dim, shards_of):
        heights = jax.random.uniform(jax.random.fold_in(jax.random.fold_in(rng, 6), dim), (shards_of,), jnp.float32, smallest / len(cuts), top_value / len(cuts))
        return jnp.repeat(jnp.exp(heights), shape[dim] // shards_of).reshape((-1,) + (1,) * (len(shape) - dim - 1))

    gain = one(*cuts[0])
    for cut in cuts[1:]:
        gain = gain * one(*cut)
    return gain


def noise(own_key, extent, width, limit, cuts=(), kind=jnp.bfloat16):
    loudness = level_of(own_key, extent, cuts, -0.22, 0.18) if cuts else 1.0
    array = jax.random.normal(own_key, extent, jnp.float32) * width * loudness
    return jnp.minimum(jnp.maximum(array, -limit), limit).astype(kind)


def setup_inputs(seed: int = 0) -> dict:
    key_of = jax.random.split(jax.random.key(seed), 9)
    hidden = noise(key_of[0], (SCENES, LEN, D), 1.0, 6.0, ((0, 16), (1, 2)))
    scan_input = noise(key_of[1], (SCENES, LEN, DI), 1.0, 6.0, ((0, 16), (1, 2)))
    grad_out = noise(key_of[2], (SCENES, LEN, DI), 1.0, 6.0, ((0, 16), (1, 2)))
    step_size = draw_step_size(jax.random.fold_in(key_of[8], 71), 0)
    proj_weight = noise(key_of[4], (D, 2 * STATE), (300 * D) ** -0.5, 0.0068359375)
    log_rate = draw_log_rate(jax.random.fold_in(key_of[8], 71), 0)
    skip_gain = jnp.clip(jax.random.uniform(key_of[6], (HEADS,), jnp.float32, 0.5, 1.5), 0.5, 1.5)
    tile_list = draw_tile_list(jax.random.fold_in(key_of[8], 71), 0)
    return {"hidden": hidden, "scan_input": scan_input, "grad_out": grad_out, "step_size": step_size, "proj_weight": proj_weight, "log_rate": log_rate, "skip_gain": skip_gain, "tile_list": tile_list}


exact_mode = lax.Precision.HIGHEST

def group_forward(carry_state, group_values, group_keys, group_query, group_step, decay_rate, gain_vector):
    block_len = group_values.shape[0]
    log_steps = group_step * decay_rate[:, None]
    running = jnp.cumsum(log_steps, axis=1)
    row_index = lax.broadcasted_iota(jnp.int32, (block_len, block_len), 0)
    col_index = lax.broadcasted_iota(jnp.int32, (block_len, block_len), 1)
    causal = row_index >= col_index
    spread = running[:, :, None] - running[:, None, :]
    decays = jnp.exp(jnp.where(causal[None], spread, -jnp.inf))
    scores = jnp.einsum('in,jn->ij', group_query, group_keys, precision=exact_mode)
    mixing = decays * scores[None] * group_step[:, None, :]
    within = jnp.einsum('hij,jhp->ihp', mixing, group_values, precision=exact_mode)
    carried = jnp.einsum('in,hpn->ihp', group_query, carry_state, precision=exact_mode) * jnp.exp(running).T[:, :, None]
    output = within + carried + gain_vector[None, :, None] * group_values
    tail_weight = jnp.exp(running[:, -1:] - running) * group_step
    weighted = group_values * tail_weight.T[:, :, None]
    fresh_state = jnp.einsum('jhp,jn->hpn', weighted, group_keys, precision=exact_mode)
    new_state = jnp.exp(running[:, -1])[:, None, None] * carry_state + fresh_state
    return (new_state, output)

def scene_output(values, projected, masked_step, decay_rate, gain_vector, present):
    values_blocks = values.reshape(GROUPS, GROUP, HEADS, HEAD_DIM)
    key_blocks = projected[:, :STATE].reshape(GROUPS, GROUP, STATE)
    query_blocks = projected[:, STATE:].reshape(GROUPS, GROUP, STATE)
    step_blocks = masked_step.reshape(HEADS, GROUPS, GROUP).transpose(1, 0, 2)

    def advance(carry_state, item):
        group_values, group_keys, group_query, group_step, group_flag = item
        new_state, output = group_forward(carry_state, group_values, group_keys, group_query, group_step, decay_rate, gain_vector)
        return (new_state, output * group_flag)
    start_state = jnp.zeros((HEADS, HEAD_DIM, STATE), jnp.float32)
    _, outputs = lax.scan(advance, start_state, (values_blocks, key_blocks, query_blocks, step_blocks, present))
    return outputs.reshape(LEN, HEADS, HEAD_DIM)

def reference(hidden, scan_input, grad_out, step_size, proj_weight, log_rate, skip_gain, tile_list):
    slot_ids = jnp.arange(CH_DEV, dtype=jnp.int32)
    listed = tile_list.reshape(SCENES, N_SEQ, CH_DEV)
    present_all = jnp.any(listed[:, :, :, None] == slot_ids[None, None, None, :], axis=2)
    present_all = present_all.reshape(SCENES, GROUPS).astype(jnp.float32)

    def per_scene(totals, item):
        activations, inputs_now, upstream, steps_now, present = item
        projected = jnp.dot(activations, proj_weight, preferred_element_type=jnp.float32)
        token_mask = jnp.repeat(present, GROUP)
        upstream_f = upstream.astype(jnp.float32).reshape(LEN, HEADS, HEAD_DIM)

        def scene_loss(values, projected_in, step_in, rate_in, gain_in):
            masked_step = step_in * token_mask[None, :]
            outputs = scene_output(values, projected_in, masked_step, -jnp.exp(rate_in), gain_in, present)
            return jnp.sum(outputs * upstream_f)
        values = inputs_now.astype(jnp.float32).reshape(LEN, HEADS, HEAD_DIM)
        grads = jax.grad(scene_loss, argnums=(0, 1, 2, 3, 4))(values, projected, steps_now, log_rate, skip_gain)
        grad_values, grad_proj, grad_steps, grad_rates, grad_gains = grads
        grad_w = jnp.dot(activations.astype(jnp.float32).T, grad_proj, precision=exact_mode)
        weight_sum, rate_sum, gain_sum = totals
        new_totals = (weight_sum + grad_w, rate_sum + grad_rates, gain_sum + grad_gains)
        return (new_totals, (grad_values.reshape(LEN, DI).astype(jnp.bfloat16), grad_steps))
    start = (jnp.zeros((D, 2 * STATE), jnp.float32), jnp.zeros((HEADS,), jnp.float32), jnp.zeros((HEADS,), jnp.float32))
    totals, per_out = lax.scan(per_scene, start, (hidden, scan_input, grad_out, step_size, present_all))
    grad_input, grad_step = per_out
    return (grad_input, grad_step, totals[0] / SCENES, totals[1] / SCENES, totals[2] / SCENES)
```

```python
import functools

import jax
import jax.numpy as jnp
from jax import lax
from jax.experimental import pallas as pl
from jax.experimental.pallas import tpu as pltpu
from jax.sharding import PartitionSpec as P

MESH = pl.DeviceIdType.MESH
EXACT = lax.Precision.HIGHEST
F32 = jnp.float32
BF16 = jnp.bfloat16
LOG2E = 1.4426950408889634
PAD = 128
SLAB = 512
VMEM = pl.BlockSpec(memory_space=pltpu.VMEM)
SMEM = pl.BlockSpec(memory_space=pltpu.SMEM)
PARAMS = pltpu.CompilerParams(vmem_limit_bytes=56 * 1024 * 1024)


def dot(a, b, dims=((1,), (0,)), precision=None):
    return lax.dot_general(a, b, (dims, ((), ())), precision=precision, preferred_element_type=F32)


def split(a):
    high = a.astype(BF16)
    return high, (a - high.astype(F32)).astype(BF16)


def to_column(row, count):
    rows = lax.broadcasted_iota(jnp.int32, (count, count), 0)
    cols = lax.broadcasted_iota(jnp.int32, (count, count), 1)
    return jnp.sum(jnp.where(rows == cols, row, 0.0), axis=1, keepdims=True)


def to_row(column, count):
    rows = lax.broadcasted_iota(jnp.int32, (count, PAD), 0)
    cols = lax.broadcasted_iota(jnp.int32, (count, PAD), 1)
    return jnp.sum(jnp.where(rows == cols, column, 0.0), axis=0, keepdims=True)


def head_spread(start, size, width):
    rows = lax.broadcasted_iota(jnp.int32, (PAD, size), 0)
    cols = lax.broadcasted_iota(jnp.int32, (PAD, size), 1) + start
    return jnp.where((cols >= rows * width) & (cols < (rows + 1) * width), 1.0, 0.0).astype(F32)


def pad_rows(a):
    return jnp.concatenate([a, jnp.zeros((PAD - a.shape[0], a.shape[1]), a.dtype)], axis=0)


def prep_kernel(
    heads, width, tile, hidden, weight, x, dy, step, log_rate, proj, tt, zs, alpha_t, l_row, l_col
):
    first = lax.axis_index("seq") == 0
    tokens = hidden.shape[0]
    state = weight.shape[1] // 2
    mask = jnp.where(tile[0, 0] == 0, 1.0, 0.0).astype(F32)
    projected = dot(hidden[...], weight[...])
    proj[...] = projected
    rate = -jnp.exp(to_column(log_rate[...], heads))
    masked = step[...] * mask
    rows = lax.broadcasted_iota(jnp.int32, (tokens, tokens), 0)
    cols = lax.broadcasted_iota(jnp.int32, (tokens, tokens), 1)
    lower = jnp.where(rows <= cols, 1.0, 0.0).astype(F32)
    running = dot(masked * rate, lower, precision=EXACT)
    alpha = jnp.where(first, jnp.exp(running[:, tokens - 1 :] - running) * masked, jnp.exp(running) * mask)
    alpha_cols = pad_rows(alpha).T
    alpha_t[...] = alpha_cols
    l_row[...] = running * LOG2E
    shifted = jnp.where(mask > 0.0, (running - jnp.log(step[...])) * LOG2E, 1e30)
    l_col[...] = pad_rows(shifted).T
    keys = jnp.where(first, projected[:, :state], projected[:, state:])
    both_keys = jnp.concatenate(split(keys), axis=1).T
    alpha_high, alpha_low = split(alpha_cols)
    both_alpha = jnp.concatenate([alpha_high, alpha_low], axis=1)
    for start in range(0, x.shape[1], SLAB):
        at = slice(start, start + SLAB)
        spread = head_spread(start, SLAB, width).astype(BF16)
        wide = dot(both_alpha, jnp.concatenate([spread, spread], axis=0))
        z = jnp.where(first, x[:, at].astype(F32), dy[:, at].astype(F32))
        scaled = (z * wide).astype(BF16)
        zs[:, at] = scaled
        both = dot(both_keys, scaled)
        tt[:, at] = both[:state] + both[state:]


def heads_kernel(heads, width, proj, x, dy, l_row, l_col, qt, dx, r_row, t_col, g):
    tokens = x.shape[0]
    state = proj.shape[1] // 2
    half = tokens // 2
    pair = 2 * width
    g[...] = dot(proj[:, :state], proj[:, state:], ((1,), (1,)), EXACT)
    qt[...] = jnp.zeros_like(qt)
    t_col[...] = jnp.zeros_like(t_col)
    rows = lax.broadcasted_iota(jnp.int32, (half, half), 0)
    cols = lax.broadcasted_iota(jnp.int32, (half, half), 1)
    causal = cols >= rows
    lane = lax.broadcasted_iota(jnp.int32, (1, pair), 1)
    lanes = lax.broadcasted_iota(jnp.int32, (tokens, PAD), 1)
    in_first = lane < width
    keep = [jnp.where(in_first, 1.0, 0.0).astype(BF16), jnp.where(in_first, 0.0, 1.0).astype(BF16)]

    @pl.loop(0, heads // 2)
    def _(k):
        at = pl.ds(pl.multiple_of(k * pair, pair), pair)
        x2 = x[:, at]
        dy2 = dy[:, at]
        columns = pltpu.roll(l_col[...], lax.rem(PAD - 2 * k, PAD), 1)
        sums = t_col[...]
        pieces = []
        for side in range(2):
            head = 2 * k + side
            l_j = columns[:, side : side + 1]
            l_i = l_row[pl.ds(head, 1), :]
            xs = x2 * keep[side]
            w_top = dot(xs[:half], dy2, ((1,), (1,)))
            w_low = dot(xs[half:], dy2[half:], ((1,), (1,)))

            def block(j, i, w, masked):
                js, at_i = slice(j * half, (j + 1) * half), slice(i * half, (i + 1) * half)
                spread = l_i[:, at_i] - l_j[js]
                if masked:
                    spread = jnp.where(causal, spread, -1e30)
                decay = jnp.exp2(spread)
                qt[js, at_i] += decay * w
                mix = decay * g[js, at_i]
                return mix, mix * w

            m00, e00 = block(0, 0, w_top[:, :half], True)
            m01, e01 = block(0, 1, w_top[:, half:], False)
            m11, e11 = block(1, 1, w_low, True)
            r_row[pl.ds(head, 1), :] = jnp.concatenate(
                [jnp.sum(e00, axis=0, keepdims=True), jnp.sum(e01 + e11, axis=0, keepdims=True)], axis=1
            )
            column = jnp.concatenate(
                [jnp.sum(e00 + e01, axis=1, keepdims=True), jnp.sum(e11, axis=1, keepdims=True)], axis=0
            )
            sums = jnp.where(lanes == head, column, sums)
            top = dot(jnp.concatenate([m00.astype(BF16), m01.astype(BF16)], axis=1), dy2)
            low = dot(m11.astype(BF16), dy2[half:])
            pieces.append((top, low))
        t_col[...] = sums
        dx[:half, at] = jnp.where(in_first, pieces[0][0], pieces[1][0])
        dx[half:, at] = jnp.where(in_first, pieces[0][1], pieces[1][1])


def finish_kernel(
    heads, width, tile, rt, proj, zs, alpha_t, qt, dx, r_row, t_col, x, dy, hidden, step, log_rate, gain,
    grad_x, grad_step, grad_w, small,
):
    first = lax.axis_index("seq") == 0
    tokens = x.shape[0]
    state = proj.shape[1] // 2
    mask = jnp.where(tile[0, 0] == 0, 1.0, 0.0).astype(F32)
    on_first = jnp.where(first, 1.0, 0.0).astype(F32)
    keys, query = proj[:, :state], proj[:, state:]
    both_keys = jnp.concatenate(split(jnp.where(first, keys, query)), axis=1)
    alpha_high, alpha_low = split(alpha_t[...] * on_first)
    both_alpha = jnp.concatenate([alpha_high, alpha_low], axis=1)
    gains = jnp.concatenate([gain[...] * mask, jnp.zeros((1, PAD - heads), F32)], axis=1)
    gains = jnp.broadcast_to(gains, (8, PAD))
    carried = jnp.zeros((tokens, PAD), F32)
    skip = jnp.zeros((8, PAD), F32)
    grad_keys = jnp.zeros((tokens, 2 * state), F32)
    for start in range(0, x.shape[1], SLAB):
        at = slice(start, start + SLAB)
        spread = head_spread(start, SLAB, width)
        spread_b = spread.astype(BF16)
        r_high, r_low = split(rt[:, at])
        back = dot(both_keys, jnp.concatenate([r_high, r_high], axis=0))
        scaled = zs[:, at]
        grad_keys += dot(scaled, jnp.concatenate([r_high, r_low], axis=0), ((1,), (1,)))
        p_high, p_low = split(scaled.astype(F32) * back)
        carried += dot(p_high, spread_b, ((1,), (1,))) + dot(p_low, spread_b, ((1,), (1,)))
        wide = dot(both_alpha, jnp.concatenate([spread_b, spread_b], axis=0))
        gain_row = dot(gains, spread, precision=EXACT)[0:1]
        out = dy[:, at].astype(F32)
        grad_x[:, at] = (dx[:, at] + wide * back + gain_row * out).astype(BF16)
        total = jnp.sum(x[:, at].astype(F32) * out, axis=0, keepdims=True)
        skip += dot(jnp.broadcast_to(total, (8, SLAB)), spread, ((1,), (1,)), EXACT)
    grad_keys = grad_keys[:, :state] + grad_keys[:, state:]
    grad_b = dot(qt[...], query, precision=EXACT) + on_first * grad_keys
    grad_c = dot(qt[...], keys, ((0,), (0,)), EXACT) + (1.0 - on_first) * grad_keys
    grad_p = jnp.concatenate([grad_b, grad_c], axis=1).astype(BF16)
    for start in range(0, hidden.shape[1], SLAB):
        grad_w[start : start + SLAB, :] = dot(hidden[:, start : start + SLAB], grad_p, ((0,), (0,)))
    rate = -jnp.exp(to_column(log_rate[...], heads))
    masked = step[...] * mask
    crossing = carried.T[:heads]
    weighted = t_col[...].T[:heads]
    sign = 1.0 - 2.0 * on_first
    grad_l = r_row[...] - weighted + sign * crossing
    rows = lax.broadcasted_iota(jnp.int32, (tokens, tokens), 0)
    cols = lax.broadcasted_iota(jnp.int32, (tokens, tokens), 1)
    upper = jnp.where(rows >= cols, 1.0, 0.0).astype(F32)
    grad_log = dot(grad_l, upper, precision=EXACT)
    grad_log += on_first * jnp.sum(crossing, axis=1, keepdims=True)
    grad_step[...] = mask * ((weighted + on_first * crossing) / step[...] + rate * grad_log)
    grad_rate = jnp.sum(grad_log * masked, axis=1, keepdims=True) * rate
    row = lax.broadcasted_iota(jnp.int32, (8, PAD), 0)
    small[...] = jnp.where(row == 0, to_row(grad_rate, heads), jnp.where(row == 1, skip * mask, 0.0))


def plan(rows, bits, order):
    steps = []
    for bit in order:
        halves = rows % 16 == 0
        rows = rows // 2 if halves else rows
        steps.append((bit, rows, halves))
    return steps


def reduce_kernel(
    bits, scenes, plans, chunk_rows, heads, w, small, out, rate_out, skip_out, acc, sacc, *rest
):
    bufs = rest[: len(plans)]
    sbuf, sems_send, sems_recv = rest[len(plans) :]
    seq, dp = lax.axis_index("seq"), lax.axis_index("dp")
    share = out.shape[0]

    def flipped(bit):
        mine = lax.rem(dp // (1 << bit), 2)
        return mine, dp + (1 - 2 * mine) * (1 << bit)

    other = 1 - seq
    barrier = pltpu.get_barrier_semaphore()
    pl.semaphore_signal(barrier, inc=1, device_id=(other, dp), device_id_type=MESH)
    for bit in range(bits):
        pl.semaphore_signal(barrier, inc=1, device_id=(seq, flipped(bit)[1]), device_id_type=MESH)
    pl.semaphore_wait(barrier, bits + 1)

    count = [0]
    pending = []

    def send(src, dst, target):
        n = count[0]
        count[0] += 1
        copy = pltpu.make_async_remote_copy(
            src_ref=src, dst_ref=dst, send_sem=sems_send.at[n], recv_sem=sems_recv.at[n],
            device_id=target, device_id_type=MESH,
        )
        copy.start()
        pending.append(copy)
        return copy

    def aligned(v):
        return pl.multiple_of(v, 8)

    bases, copies = [], []
    base = 0
    for c, rows in enumerate(chunk_rows):
        bases.append(base)
        copies.append(
            send(w.at[pl.ds(aligned(other * share + base), rows)], bufs[c].at[pl.ds(0, rows)], (other, dp))
        )
        base += rows
    scopy = send(small, sbuf.at[0], (other, dp))

    starts = [None] * len(plans)
    offsets = [0] * len(plans)
    sizes = list(chunk_rows)
    history = [[] for _ in plans]
    for c, rows in enumerate(chunk_rows):
        copies[c].wait_recv()
        mine = w[pl.ds(aligned(seq * share + bases[c]), rows), :]
        acc[pl.ds(bases[c], rows), :] = mine + bufs[c][0:rows, :]
        starts[c] = bases[c]
        offsets[c] = rows
        bit, kept, halves = plans[c][0]
        side, peer = flipped(bit)
        copies[c] = start_step(send, aligned, acc, bufs, c, starts, offsets, bit, kept, halves, side, peer, seq, history)
    scopy.wait_recv()
    sacc[0] = small[...] + sbuf[0]
    scopy = send(sacc.at[0], sbuf.at[1], (seq, flipped(0)[1]))

    for s in range(bits):
        for c in range(len(plans)):
            bit, kept, halves = plans[c][s]
            copies[c].wait_recv()
            if not halves:
                copies[c].wait_send()
                pending[:] = [p for p in pending if p is not copies[c]]
            here = pl.ds(starts[c], kept)
            acc[here, :] = acc[here, :] + bufs[c][offsets[c] - kept : offsets[c], :]
            if s + 1 < bits:
                bit, kept, halves = plans[c][s + 1]
                side, peer = flipped(bit)
                copies[c] = start_step(
                    send, aligned, acc, bufs, c, starts, offsets, bit, kept, halves, side, peer, seq, history
                )
        scopy.wait_recv()
        sacc[s + 1] = sacc[s] + sbuf[s + 1]
        if s + 1 < bits:
            scopy = send(sacc.at[s + 1], sbuf.at[s + 2], (seq, flipped(s + 1)[1]))

    scale = 1.0 / scenes
    gathers = [None] * len(plans)
    trail = [[h for h in history[c] if h[3]] for c in range(len(plans))]
    longest = max(len(t) for t in trail)

    def gather(c, n):
        bit, kept, side, _, start = trail[c][len(trail[c]) - 1 - n]
        peer = flipped(bit)[1]
        region = out.at[pl.ds(start, kept)]
        return send(region, region, (seq, peer))

    for c in range(len(plans)):
        kept = plans[c][-1][1]
        here = pl.ds(starts[c], kept)
        out[here, :] = acc[here, :] * scale
        gathers[c] = gather(c, 0)
    total = sacc[bits] * scale
    total = jnp.where(seq == 0, total, pltpu.roll(total, PAD - heads // 2, 1))
    rate_out[...] = total[0:1, : heads // 2]
    skip_out[...] = total[1:2, : heads // 2]
    for n in range(longest):
        for c in range(len(plans)):
            if n < len(trail[c]):
                gathers[c].wait_recv()
                if n + 1 < len(trail[c]):
                    gathers[c] = gather(c, n + 1)
    for copy in pending:
        copy.wait_send()


def start_step(send, aligned, acc, bufs, c, starts, offsets, bit, kept, halves, side, peer, seq, history):
    begin = starts[c]
    if halves:
        source = aligned(begin + (1 - side) * kept)
        starts[c] = aligned(begin + side * kept)
    else:
        source = begin
    offset = offsets[c]
    offsets[c] = offset + kept
    history[c].append((bit, kept, side, halves, starts[c]))
    return send(acc.at[pl.ds(source, kept)], bufs[c].at[pl.ds(offset, kept)], (seq, peer))


def reduce_all(grad_w, small, scenes, heads):
    seqs = lax.axis_size("seq")
    bits = scenes.bit_length() - 1
    rows = grad_w.shape[0] // seqs
    low = rows // 5
    chunk_rows = (2 * low, 2 * low, rows - 4 * low)
    natural = list(range(bits))
    orders = (natural, [1, 0] + natural[2:], natural[2:] + natural[:2])
    plans = [plan(r, bits, o) for r, o in zip(chunk_rows, orders)]
    scratch = [pltpu.VMEM((rows, grad_w.shape[1]), F32), pltpu.VMEM((bits + 1, 8, PAD), F32)]
    for r, steps in zip(chunk_rows, plans):
        scratch.append(pltpu.VMEM((r + sum(k for _, k, _ in steps), grad_w.shape[1]), F32))
    scratch.append(pltpu.VMEM((bits + 1, 8, PAD), F32))
    copies = len(plans) * (1 + 2 * bits) + bits + 1
    scratch += [pltpu.SemaphoreType.DMA((copies,)), pltpu.SemaphoreType.DMA((copies,))]
    return pl.pallas_call(
        functools.partial(reduce_kernel, bits, scenes, plans, chunk_rows, heads),
        out_shape=(
            jax.ShapeDtypeStruct((rows, grad_w.shape[1]), F32),
            jax.ShapeDtypeStruct((1, heads // seqs), F32),
            jax.ShapeDtypeStruct((1, heads // seqs), F32),
        ),
        in_specs=[VMEM, VMEM],
        out_specs=(VMEM, VMEM, VMEM),
        scratch_shapes=scratch,
        compiler_params=pltpu.CompilerParams(
            collective_id=0, has_side_effects=True, vmem_limit_bytes=40 * 1024 * 1024
        ),
    )(grad_w, small)


def shards(hidden, scan_input, grad_out, step_size, proj_weight, log_rate, skip_gain, tile_list):
    tokens, inner = scan_input.shape[1:]
    model, two_state = proj_weight.shape
    heads = log_rate.shape[0]
    width = inner // heads
    scenes = lax.axis_size("dp")
    x, dy, acts, step = scan_input[0], grad_out[0], hidden[0], step_size[0]
    log_rate, gain = log_rate[None], skip_gain[None]

    def shape(*dims, dtype=F32):
        return jax.ShapeDtypeStruct(dims, dtype)

    proj, tt, zs, alpha_t, l_row, l_col = pl.pallas_call(
        functools.partial(prep_kernel, heads, width),
        out_shape=(
            shape(tokens, two_state), shape(two_state // 2, inner), shape(tokens, inner, dtype=BF16),
            shape(tokens, PAD), shape(heads, tokens), shape(tokens, PAD),
        ),
        in_specs=[SMEM] + [VMEM] * 6,
        out_specs=(VMEM,) * 6,
        compiler_params=PARAMS,
        name="prep",
    )(tile_list, acts, proj_weight, x, dy, step, log_rate)
    rt = lax.ppermute(tt, "seq", [(0, 1), (1, 0)])
    qt, dx, r_row, t_col = pl.pallas_call(
        functools.partial(heads_kernel, heads, width),
        out_shape=(
            shape(tokens, tokens), shape(tokens, inner), shape(heads, tokens), shape(tokens, PAD),
        ),
        in_specs=[VMEM] * 5,
        out_specs=(VMEM,) * 4,
        scratch_shapes=[pltpu.VMEM((tokens, tokens), F32)],
        compiler_params=PARAMS,
        cost_estimate=pl.CostEstimate(flops=8 * 10**9, bytes_accessed=8 * 10**6, transcendentals=3 * 10**6),
        name="heads",
    )(proj, x, dy, l_row, l_col)
    grad_x, grad_step, grad_w, small = pl.pallas_call(
        functools.partial(finish_kernel, heads, width),
        out_shape=(
            shape(tokens, inner, dtype=BF16), shape(heads, tokens), shape(model, two_state), shape(8, PAD),
        ),
        in_specs=[SMEM] + [VMEM] * 14,
        out_specs=(VMEM,) * 4,
        compiler_params=PARAMS,
        name="finish",
    )(tile_list, rt, proj, zs, alpha_t, qt, dx, r_row, t_col, x, dy, acts, step, log_rate, gain)
    summed, rates, gains = reduce_all(grad_w, small, scenes, heads)
    return grad_x[None], grad_step[None], summed, rates[0], gains[0]


def solution(mesh):
    in_specs = (
        P("dp", "seq", None),
        P("dp", "seq", None),
        P("dp", "seq", None),
        P("dp", None, "seq"),
        P(),
        P(),
        P(),
        P("dp", "seq"),
    )
    out_specs = (P("dp", "seq", None), P("dp", None, "seq"), P("seq", None), P("seq"), P("seq"))
    return jax.shard_map(shards, mesh=mesh, in_specs=in_specs, out_specs=out_specs, check_vma=False)
```

```python
import functools

import jax
import jax.numpy as jnp
from jax import lax
from jax.experimental import pallas as pl
from jax.experimental.pallas import tpu as pltpu
from jax.sharding import PartitionSpec as P

MESH = pl.DeviceIdType.MESH
EXACT = lax.Precision.HIGHEST
F32 = jnp.float32
BF16 = jnp.bfloat16
LOG2E = 1.4426950408889634
PAD = 128
SLAB = 512
ORDER = (2, 0, 1)
QUOTAS = (3, 4, 1, 3, 2, 1, 3, 1, 1, 1, 1, 1, 2, 2, 1)
VMEM = pl.BlockSpec(memory_space=pltpu.VMEM)
SMEM = pl.BlockSpec(memory_space=pltpu.SMEM)
PARAMS = pltpu.CompilerParams(vmem_limit_bytes=56 * 1024 * 1024)


def dot(a, b, dims=((1,), (0,)), precision=None):
    return lax.dot_general(a, b, (dims, ((), ())), precision=precision, preferred_element_type=F32)


def split(a):
    high = a.astype(BF16)
    return high, (a - high.astype(F32)).astype(BF16)


def to_column(row, count):
    rows = lax.broadcasted_iota(jnp.int32, (count, count), 0)
    cols = lax.broadcasted_iota(jnp.int32, (count, count), 1)
    return jnp.sum(jnp.where(rows == cols, row, 0.0), axis=1, keepdims=True)


def to_row(column, count):
    rows = lax.broadcasted_iota(jnp.int32, (count, PAD), 0)
    cols = lax.broadcasted_iota(jnp.int32, (count, PAD), 1)
    return jnp.sum(jnp.where(rows == cols, column, 0.0), axis=0, keepdims=True)


def head_spread(start, size, width):
    rows = lax.broadcasted_iota(jnp.int32, (PAD, size), 0)
    cols = lax.broadcasted_iota(jnp.int32, (PAD, size), 1) + start
    return jnp.where((cols >= rows * width) & (cols < (rows + 1) * width), 1.0, 0.0).astype(F32)


def pad_rows(a):
    return jnp.concatenate([a, jnp.zeros((PAD - a.shape[0], a.shape[1]), a.dtype)], axis=0)


def prep_kernel(
    heads, width, tile, hidden, weight, x, dy, step, log_rate, proj, tt, zs, alpha_t, l_row, l_col
):
    first = lax.axis_index("seq") == 0
    tokens = hidden.shape[0]
    state = weight.shape[1] // 2
    mask = jnp.where(tile[0, 0] == 0, 1.0, 0.0).astype(F32)
    projected = dot(hidden[...], weight[...])
    proj[...] = projected
    rate = -jnp.exp(to_column(log_rate[...], heads))
    masked = step[...] * mask
    rows = lax.broadcasted_iota(jnp.int32, (tokens, tokens), 0)
    cols = lax.broadcasted_iota(jnp.int32, (tokens, tokens), 1)
    lower = jnp.where(rows <= cols, 1.0, 0.0).astype(F32)
    running = dot(masked * rate, lower, precision=EXACT)
    alpha = jnp.where(first, jnp.exp(running[:, tokens - 1 :] - running) * masked, jnp.exp(running) * mask)
    alpha_cols = pad_rows(alpha).T
    alpha_t[...] = alpha_cols
    l_row[...] = running * LOG2E
    shifted = jnp.where(mask > 0.0, (running - jnp.log(step[...])) * LOG2E, 1e30)
    l_col[...] = pad_rows(shifted).T
    keys = jnp.where(first, projected[:, :state], projected[:, state:])
    both_keys = jnp.concatenate(split(keys), axis=1).T
    alpha_high, alpha_low = split(alpha_cols)
    both_alpha = jnp.concatenate([alpha_high, alpha_low], axis=1)
    for start in range(0, x.shape[1], SLAB):
        at = slice(start, start + SLAB)
        spread = head_spread(start, SLAB, width).astype(BF16)
        wide = dot(both_alpha, jnp.concatenate([spread, spread], axis=0))
        z = jnp.where(first, x[:, at].astype(F32), dy[:, at].astype(F32))
        scaled, scaled_low = split(z * wide)
        zs[:, at] = scaled
        both = dot(both_keys, scaled) + dot(both_keys, scaled_low)
        tt[:, at] = both[:state] + both[state:]


def pair_parts(k, heads, width, x, dy, l_row, l_col):
    tokens = x.shape[0]
    half = tokens // 2
    pair = 2 * width
    rows = lax.broadcasted_iota(jnp.int32, (half, half), 0)
    cols = lax.broadcasted_iota(jnp.int32, (half, half), 1)
    causal = cols >= rows
    in_first = lax.broadcasted_iota(jnp.int32, (1, pair), 1) < width
    keep = [jnp.where(in_first, 1.0, 0.0).astype(BF16), jnp.where(in_first, 0.0, 1.0).astype(BF16)]
    at = pl.ds(pl.multiple_of(k * pair, pair), pair)
    x2 = x[:, at]
    dy2 = dy[:, at]
    columns = pltpu.roll(l_col[...], lax.rem(PAD - 2 * k, PAD), 1)
    sides = []
    for side in range(2):
        l_j = columns[:, side : side + 1]
        l_i = l_row[pl.ds(2 * k + side, 1), :]
        xs = x2 * keep[side]
        w_top = dot(xs[:half], dy2, ((1,), (1,)))
        w_low = dot(xs[half:], dy2[half:], ((1,), (1,)))
        d00 = jnp.exp2(jnp.where(causal, l_i[:, :half] - l_j[:half], -1e30))
        d01 = jnp.exp2(l_i[:, half:] - l_j[:half])
        d11 = jnp.exp2(jnp.where(causal, l_i[:, half:] - l_j[half:], -1e30))
        sides.append(((d00, w_top[:, :half]), (d01, w_top[:, half:]), (d11, w_low)))
    return at, dy2, in_first, sides


def heads_kernel(heads, width, x, dy, l_row, l_col, qt):
    half = x.shape[0] // 2
    qt[...] = jnp.zeros_like(qt)

    @pl.loop(0, heads // 2)
    def _(k):
        _, _, _, sides = pair_parts(k, heads, width, x, dy, l_row, l_col)
        for n, (j, i) in enumerate(((0, 0), (0, 1), (1, 1))):
            js, at_i = slice(j * half, (j + 1) * half), slice(i * half, (i + 1) * half)
            (d_a, w_a), (d_b, w_b) = sides[0][n], sides[1][n]
            qt[js, at_i] += d_a * w_a + d_b * w_b


def one_pair(k, heads, width, x, dy, l_row, l_col, g, dx, r_row, t_col):
    tokens = x.shape[0]
    half = tokens // 2
    lanes = lax.broadcasted_iota(jnp.int32, (tokens, PAD), 1)
    at, dy2, in_first, sides = pair_parts(k, heads, width, x, dy, l_row, l_col)
    sums = t_col[...]
    pieces = []
    for side in range(2):
        head = 2 * k + side
        (d00, w00), (d01, w01), (d11, w11) = sides[side]
        m00, m01, m11 = d00 * g[:half, :half], d01 * g[:half, half:], d11 * g[half:, half:]
        e00, e01, e11 = m00 * w00, m01 * w01, m11 * w11
        r_row[pl.ds(head, 1), :] = jnp.concatenate(
            [jnp.sum(e00, axis=0, keepdims=True), jnp.sum(e01 + e11, axis=0, keepdims=True)], axis=1
        )
        column = jnp.concatenate(
            [jnp.sum(e00 + e01, axis=1, keepdims=True), jnp.sum(e11, axis=1, keepdims=True)], axis=0
        )
        sums = jnp.where(lanes == head, column, sums)
        top_high, top_low = split(jnp.concatenate([m00, m01], axis=1))
        low_high, low_low = split(m11)
        top = dot(top_high, dy2) + dot(top_low, dy2)
        low = dot(low_high, dy2[half:]) + dot(low_low, dy2[half:])
        pieces.append((top, low))
    t_col[...] = sums
    dx[:half, at] = jnp.where(in_first, pieces[0][0], pieces[1][0])
    dx[half:, at] = jnp.where(in_first, pieces[0][1], pieces[1][1])


def plan(rows, bits, order):
    steps = []
    for bit in order:
        halves = rows % 16 == 0
        rows = rows // 2 if halves else rows
        steps.append((bit, rows, halves))
    return steps


def reduce_kernel(
    bits, scenes, plans, chunk_rows, heads, width,
    tile, rt, proj, zs, alpha_t, qt, hidden, l_row, l_col, step, log_rate, gain, x_hbm, dy_hbm,
    grad_x, grad_step, out, rate_out, skip_out,
    x, dy, dx, r_row, t_col, g, w, small, acc, sacc, *rest
):
    bufs = rest[: len(plans)]
    sbuf, sems_send, sems_recv, sems_load = rest[len(plans) :]
    seq, dp = lax.axis_index("seq"), lax.axis_index("dp")
    share = out.shape[0]
    tokens = x.shape[0]
    state = proj.shape[1] // 2

    def flipped(bit):
        mine = lax.rem(dp // (1 << bit), 2)
        return mine, dp + (1 - 2 * mine) * (1 << bit)

    other = 1 - seq
    loads = [
        pltpu.make_async_copy(x_hbm, x, sems_load.at[0]),
        pltpu.make_async_copy(dy_hbm, dy, sems_load.at[1]),
    ]
    for load in loads:
        load.start()
    barrier = pltpu.get_barrier_semaphore()
    pl.semaphore_signal(barrier, inc=1, device_id=(other, dp), device_id_type=MESH)
    for bit in range(bits):
        pl.semaphore_signal(barrier, inc=1, device_id=(seq, flipped(bit)[1]), device_id_type=MESH)

    mask = jnp.where(tile[0, 0] == 0, 1.0, 0.0).astype(F32)
    on_first = jnp.where(seq == 0, 1.0, 0.0).astype(F32)
    keys, query = proj[:, :state], proj[:, state:]
    grad_keys = jnp.zeros((tokens, 2 * state), F32)
    for start in range(0, zs.shape[1], SLAB):
        at = slice(start, start + SLAB)
        grad_keys += dot(zs[:, at], jnp.concatenate(split(rt[:, at]), axis=0), ((1,), (1,)))
    grad_keys = grad_keys[:, :state] + grad_keys[:, state:]
    grad_b = dot(qt[...], query, precision=EXACT) + on_first * grad_keys
    grad_c = dot(qt[...], keys, ((0,), (0,)), EXACT) + (1.0 - on_first) * grad_keys
    grad_p = jnp.concatenate([grad_b, grad_c], axis=1).astype(BF16)

    count = [0]
    pending = []

    def send(src, dst, target):
        n = count[0]
        count[0] += 1
        copy = pltpu.make_async_remote_copy(
            src_ref=src, dst_ref=dst, send_sem=sems_send.at[n], recv_sem=sems_recv.at[n],
            device_id=target, device_id_type=MESH,
        )
        copy.start()
        pending.append(copy)
        return copy

    def aligned(v):
        return pl.multiple_of(v, 8)

    def weight_rows(start, rows):
        w[pl.ds(aligned(start), rows), :] = dot(
            hidden[:, pl.ds(pl.multiple_of(start, PAD), rows)], grad_p, ((0,), (0,))
        )

    chunks = ORDER
    bases = [sum(chunk_rows[:c]) for c in range(len(plans))]
    copies = [None] * len(plans)
    for n, c in enumerate(chunks):
        rows = chunk_rows[c]
        weight_rows(other * share + bases[c], rows)
        if n == 0:
            pl.semaphore_wait(barrier, bits + 1)
        copies[c] = send(
            w.at[pl.ds(aligned(other * share + bases[c]), rows)], bufs[c].at[pl.ds(0, rows)], (other, dp)
        )

    pair_args = (heads, width, x, dy, l_row, l_col, g, dx, r_row, t_col)
    scale = 1.0 / scenes
    done_pairs = [0]
    done_slabs = [0]
    slabs = zs.shape[1] // SLAB
    terms = {"carried": jnp.zeros((tokens, PAD), F32), "skip": jnp.zeros((8, PAD), F32)}
    light = [-1, None]

    def run_pairs(n):
        lo = done_pairs[0]
        hi = min(lo + n, heads // 2)
        done_pairs[0] = hi
        if lo == 0 and hi > 0:
            g[...] = dot(keys, query, ((1,), (1,)), EXACT)
            t_col[...] = jnp.zeros_like(t_col)
            for load in loads:
                load.wait()
        if hi > lo:

            @pl.loop(lo, hi)
            def _(k):
                one_pair(k, *pair_args)

    def run_slabs(n):
        both_keys = jnp.concatenate(split(jnp.where(seq == 0, keys, query)), axis=1)
        alpha_high, alpha_low = split(alpha_t[...] * on_first)
        both_alpha = jnp.concatenate([alpha_high, alpha_low], axis=1)
        gains = jnp.concatenate([gain[...] * mask, jnp.zeros((1, PAD - heads), F32)], axis=1)
        gains = jnp.broadcast_to(gains, (8, PAD))
        for _ in range(n):
            if done_slabs[0] >= slabs:
                return
            start = done_slabs[0] * SLAB
            done_slabs[0] += 1
            at = slice(start, start + SLAB)
            spread = head_spread(start, SLAB, width)
            spread_b = spread.astype(BF16)
            r_high, r_low = split(rt[:, at])
            back = dot(both_keys, jnp.concatenate([r_high, r_high], axis=0)) + dot(both_keys[:, :state], r_low)
            p_high, p_low = split(zs[:, at].astype(F32) * back)
            terms["carried"] += dot(p_high, spread_b, ((1,), (1,))) + dot(p_low, spread_b, ((1,), (1,)))
            wide = dot(both_alpha, jnp.concatenate([spread_b, spread_b], axis=0))
            gain_row = dot(gains, spread, precision=EXACT)[0:1]
            top = dy[:, at].astype(F32)
            grad_x[:, at] = (dx[:, at] + wide * back + gain_row * top).astype(BF16)
            total = jnp.sum(x[:, at].astype(F32) * top, axis=0, keepdims=True)
            terms["skip"] += dot(jnp.broadcast_to(total, (8, SLAB)), spread, ((1,), (1,)), EXACT)

    def run_last():
        rate = -jnp.exp(to_column(log_rate[...], heads))
        crossing = terms["carried"].T[:heads]
        weighted = t_col[...].T[:heads]
        sign = 1.0 - 2.0 * on_first
        grad_l = r_row[...] - weighted + sign * crossing
        rows = lax.broadcasted_iota(jnp.int32, (tokens, tokens), 0)
        cols = lax.broadcasted_iota(jnp.int32, (tokens, tokens), 1)
        upper = jnp.where(rows >= cols, 1.0, 0.0).astype(F32)
        grad_log = dot(grad_l, upper, precision=EXACT)
        grad_log += on_first * jnp.sum(crossing, axis=1, keepdims=True)
        grad_step[...] = mask * ((weighted + on_first * crossing) / step[...] + rate * grad_log)
        grad_rate = jnp.sum(grad_log * (step[...] * mask), axis=1, keepdims=True) * rate
        row = lax.broadcasted_iota(jnp.int32, (8, PAD), 0)
        small[...] = jnp.where(row == 0, to_row(grad_rate, heads), jnp.where(row == 1, terms["skip"] * mask, 0.0))

    def advance_small():
        stage = light[0]
        if stage > bits:
            return
        if stage >= 0:
            light[1].wait_recv()
            sacc[stage] = (small[...] if stage == 0 else sacc[stage - 1]) + sbuf[stage]
        light[0] = stage = stage + 1
        if stage == 0:
            light[1] = send(small, sbuf.at[0], (other, dp))
        elif stage <= bits:
            light[1] = send(sacc.at[stage - 1], sbuf.at[stage], (seq, flipped(stage - 1)[1]))

    quotas = list(QUOTAS)

    def tick():
        n = quotas.pop(0) if quotas else 1
        if done_pairs[0] < heads // 2:
            run_pairs(n)
        elif done_slabs[0] < slabs:
            run_slabs(n)
            if done_slabs[0] == slabs:
                run_last()
                advance_small()
        else:
            advance_small()

    starts = list(bases)
    offsets = list(chunk_rows)
    history = [[] for _ in plans]

    def start_step(c, s):
        bit, kept, halves = plans[c][s]
        side, peer = flipped(bit)
        begin = starts[c]
        source = begin
        if halves:
            source = aligned(begin + (1 - side) * kept)
            starts[c] = aligned(begin + side * kept)
        offset = offsets[c]
        offsets[c] = offset + kept
        history[c].append((bit, kept, halves, starts[c]))
        copies[c] = send(acc.at[pl.ds(source, kept)], bufs[c].at[pl.ds(offset, kept)], (seq, peer))

    for c in chunks:
        weight_rows(seq * share + bases[c], chunk_rows[c])
    for c in chunks:
        rows = chunk_rows[c]
        copies[c].wait_recv()
        mine = w[pl.ds(aligned(seq * share + bases[c]), rows), :]
        acc[pl.ds(bases[c], rows), :] = mine + bufs[c][0:rows, :]
        start_step(c, 0)

    for s in range(bits):
        for c in chunks:
            tick()
            kept, halves = plans[c][s][1:]
            copies[c].wait_recv()
            if not halves:
                copies[c].wait_send()
                pending[:] = [p for p in pending if p is not copies[c]]
            here = pl.ds(starts[c], kept)
            acc[here, :] = acc[here, :] + bufs[c][offsets[c] - kept : offsets[c], :]
            if s + 1 < bits:
                start_step(c, s + 1)
            else:
                out[here, :] = acc[here, :] * scale

    trail = [[h for h in reversed(history[c]) if h[2]] for c in range(len(plans))]

    def gather(c, n):
        bit, kept, _, start = trail[c][n]
        region = out.at[pl.ds(start, kept)]
        return send(region, region, (seq, flipped(bit)[1]))

    for c in chunks:
        copies[c] = gather(c, 0)
    for n in range(max(len(t) for t in trail)):
        for c in chunks:
            if n < len(trail[c]):
                tick()
                copies[c].wait_recv()
                if n + 1 < len(trail[c]):
                    copies[c] = gather(c, n + 1)
    while light[0] <= bits:
        tick()
    total = sacc[bits] * scale
    total = jnp.where(seq == 0, total, pltpu.roll(total, PAD - heads // 2, 1))
    rate_out[...] = total[0:1, : heads // 2]
    skip_out[...] = total[1:2, : heads // 2]
    for copy in pending:
        copy.wait_send()


def reduce_all(scenes, heads, width, args):
    rt, hidden = args[1], args[6]
    tokens, model = hidden.shape
    inner = rt.shape[1]
    two_state = 2 * rt.shape[0]
    seqs = lax.axis_size("seq")
    bits = scenes.bit_length() - 1
    rows = model // seqs
    low = rows // 5
    chunk_rows = (2 * low, 2 * low, rows - 4 * low)
    natural = list(range(bits))
    orders = (natural, [1, 0] + natural[2:], natural[2:] + natural[:2])
    plans = [plan(r, bits, o) for r, o in zip(chunk_rows, orders)]
    scratch = [
        pltpu.VMEM((tokens, inner), BF16), pltpu.VMEM((tokens, inner), BF16), pltpu.VMEM((tokens, inner), F32),
        pltpu.VMEM((heads, tokens), F32), pltpu.VMEM((tokens, PAD), F32), pltpu.VMEM((tokens, tokens), F32),
        pltpu.VMEM((model, two_state), F32), pltpu.VMEM((8, PAD), F32),
        pltpu.VMEM((rows, two_state), F32), pltpu.VMEM((bits + 1, 8, PAD), F32),
    ]
    for r, steps in zip(chunk_rows, plans):
        scratch.append(pltpu.VMEM((r + sum(k for _, k, _ in steps), two_state), F32))
    scratch.append(pltpu.VMEM((bits + 1, 8, PAD), F32))
    copies = len(plans) * (1 + 2 * bits) + bits + 1
    scratch += [pltpu.SemaphoreType.DMA((copies,)), pltpu.SemaphoreType.DMA((copies,)), pltpu.SemaphoreType.DMA((2,))]
    return pl.pallas_call(
        functools.partial(reduce_kernel, bits, scenes, plans, chunk_rows, heads, width),
        out_shape=(
            jax.ShapeDtypeStruct((tokens, inner), BF16),
            jax.ShapeDtypeStruct((heads, tokens), F32),
            jax.ShapeDtypeStruct((rows, two_state), F32),
            jax.ShapeDtypeStruct((1, heads // seqs), F32),
            jax.ShapeDtypeStruct((1, heads // seqs), F32),
        ),
        in_specs=[SMEM] + [VMEM] * 11 + [pl.BlockSpec(memory_space=pl.ANY)] * 2,
        out_specs=(VMEM,) * 5,
        scratch_shapes=scratch,
        compiler_params=pltpu.CompilerParams(
            collective_id=0, has_side_effects=True, vmem_limit_bytes=48 * 1024 * 1024
        ),
        name="finish",
    )(*args)


def shards(hidden, scan_input, grad_out, step_size, proj_weight, log_rate, skip_gain, tile_list):
    tokens, inner = scan_input.shape[1:]
    model, two_state = proj_weight.shape
    heads = log_rate.shape[0]
    width = inner // heads
    scenes = lax.axis_size("dp")
    x, dy, acts, step = scan_input[0], grad_out[0], hidden[0], step_size[0]
    log_rate, gain = log_rate[None], skip_gain[None]

    def shape(*dims, dtype=F32):
        return jax.ShapeDtypeStruct(dims, dtype)

    proj, tt, zs, alpha_t, l_row, l_col = pl.pallas_call(
        functools.partial(prep_kernel, heads, width),
        out_shape=(
            shape(tokens, two_state), shape(two_state // 2, inner), shape(tokens, inner, dtype=BF16),
            shape(tokens, PAD), shape(heads, tokens), shape(tokens, PAD),
        ),
        in_specs=[SMEM] + [VMEM] * 6,
        out_specs=(VMEM,) * 6,
        compiler_params=PARAMS,
        name="prep",
    )(tile_list, acts, proj_weight, x, dy, step, log_rate)
    rt = lax.ppermute(tt, "seq", [(0, 1), (1, 0)])
    qt = pl.pallas_call(
        functools.partial(heads_kernel, heads, width),
        out_shape=shape(tokens, tokens),
        in_specs=[VMEM] * 4,
        out_specs=VMEM,
        compiler_params=PARAMS,
        cost_estimate=pl.CostEstimate(flops=8 * 10**9, bytes_accessed=8 * 10**6, transcendentals=3 * 10**6),
        name="heads",
    )(x, dy, l_row, l_col)
    args = (tile_list, rt, proj, zs, alpha_t, qt, acts, l_row, l_col, step, log_rate, gain, x, dy)
    grad_x, grad_step, summed, rates, gains = reduce_all(scenes, heads, width, args)
    return grad_x[None], grad_step[None], summed, rates[0], gains[0]


def solution(mesh):
    in_specs = (
        P("dp", "seq", None),
        P("dp", "seq", None),
        P("dp", "seq", None),
        P("dp", None, "seq"),
        P(),
        P(),
        P(),
        P("dp", "seq"),
    )
    out_specs = (P("dp", "seq", None), P("dp", None, "seq"), P("seq", None), P("seq"), P("seq"))
    return jax.shard_map(shards, mesh=mesh, in_specs=in_specs, out_specs=out_specs, check_vma=False)
```

```python
import functools

import jax
import jax.numpy as jnp
from jax import lax
from jax.experimental import pallas as pl
from jax.experimental.pallas import tpu as pltpu
from jax.sharding import PartitionSpec as P

MESH = pl.DeviceIdType.MESH
EXACT = lax.Precision.HIGHEST
F32 = jnp.float32
BF16 = jnp.bfloat16
LOG2E = 1.4426950408889634
PAD = 128
SLAB = 512
QUOTAS = (1, 5, 1, 0, 2, 1, 0, 1, 1, 0, 3, 1, 0, 2, 1, 1, 3, 2, 1, 0, 1, 1, 1, 1, 1)
VMEM = pl.BlockSpec(memory_space=pltpu.VMEM)
SMEM = pl.BlockSpec(memory_space=pltpu.SMEM)


def dot(a, b, dims=((1,), (0,)), precision=None):
    return lax.dot_general(a, b, (dims, ((), ())), precision=precision, preferred_element_type=F32)


def split(a):
    high = a.astype(BF16)
    return high, (a - high.astype(F32)).astype(BF16)


def to_column(row, count):
    rows = lax.broadcasted_iota(jnp.int32, (count, count), 0)
    cols = lax.broadcasted_iota(jnp.int32, (count, count), 1)
    return jnp.sum(jnp.where(rows == cols, row, 0.0), axis=1, keepdims=True)


def to_row(column, count):
    rows = lax.broadcasted_iota(jnp.int32, (count, PAD), 0)
    cols = lax.broadcasted_iota(jnp.int32, (count, PAD), 1)
    return jnp.sum(jnp.where(rows == cols, column, 0.0), axis=0, keepdims=True)


def head_spread(start, size, width):
    rows = lax.broadcasted_iota(jnp.int32, (PAD, size), 0)
    cols = lax.broadcasted_iota(jnp.int32, (PAD, size), 1) + start
    return jnp.where((cols >= rows * width) & (cols < (rows + 1) * width), 1.0, 0.0).astype(F32)


def pad_rows(a):
    return jnp.concatenate([a, jnp.zeros((PAD - a.shape[0], a.shape[1]), a.dtype)], axis=0)


def pair_parts(k, heads, width, x, dy, l_row, l_col):
    tokens = x.shape[0]
    half = tokens // 2
    pair = 2 * width
    rows = lax.broadcasted_iota(jnp.int32, (half, half), 0)
    cols = lax.broadcasted_iota(jnp.int32, (half, half), 1)
    causal = cols >= rows
    in_first = lax.broadcasted_iota(jnp.int32, (1, pair), 1) < width
    keep = [jnp.where(in_first, 1.0, 0.0).astype(BF16), jnp.where(in_first, 0.0, 1.0).astype(BF16)]
    at = pl.ds(pl.multiple_of(k * pair, pair), pair)
    x2 = x[:, at]
    dy2 = dy[:, at]
    columns = pltpu.roll(l_col[...], lax.rem(PAD - 2 * k, PAD), 1)
    sides = []
    for side in range(2):
        l_j = columns[:, side : side + 1]
        l_i = l_row[pl.ds(2 * k + side, 1), :]
        xs = x2 * keep[side]
        w_top = dot(xs[:half], dy2, ((1,), (1,)))
        w_low = dot(xs[half:], dy2[half:], ((1,), (1,)))
        d00 = jnp.exp2(jnp.where(causal, l_i[:, :half] - l_j[:half], -1e30))
        d01 = jnp.exp2(l_i[:, half:] - l_j[:half])
        d11 = jnp.exp2(jnp.where(causal, l_i[:, half:] - l_j[half:], -1e30))
        sides.append(((d00, w_top[:, :half]), (d01, w_top[:, half:]), (d11, w_low)))
    return at, dy2, in_first, sides


def heads_part(heads, width, x, dy, l_row, l_col, qt):
    half = x.shape[0] // 2
    qt[...] = jnp.zeros_like(qt)

    @pl.loop(0, heads // 2)
    def _(k):
        _, _, _, sides = pair_parts(k, heads, width, x, dy, l_row, l_col)
        for n, (j, i) in enumerate(((0, 0), (0, 1), (1, 1))):
            js, at_i = slice(j * half, (j + 1) * half), slice(i * half, (i + 1) * half)
            (d_a, w_a), (d_b, w_b) = sides[0][n], sides[1][n]
            qt[js, at_i] += d_a * w_a + d_b * w_b


def one_pair(k, heads, width, x, dy, l_row, l_col, g, dx, r_row, t_col):
    tokens = x.shape[0]
    half = tokens // 2
    lanes = lax.broadcasted_iota(jnp.int32, (tokens, PAD), 1)
    at, dy2, in_first, sides = pair_parts(k, heads, width, x, dy, l_row, l_col)
    sums = t_col[...]
    pieces = []
    for side in range(2):
        head = 2 * k + side
        (d00, w00), (d01, w01), (d11, w11) = sides[side]
        m00, m01, m11 = d00 * g[:half, :half], d01 * g[:half, half:], d11 * g[half:, half:]
        e00, e01, e11 = m00 * w00, m01 * w01, m11 * w11
        r_row[pl.ds(head, 1), :] = jnp.concatenate(
            [jnp.sum(e00, axis=0, keepdims=True), jnp.sum(e01 + e11, axis=0, keepdims=True)], axis=1
        )
        column = jnp.concatenate(
            [jnp.sum(e00 + e01, axis=1, keepdims=True), jnp.sum(e11, axis=1, keepdims=True)], axis=0
        )
        sums = jnp.where(lanes == head, column, sums)
        top_high, top_low = split(jnp.concatenate([m00, m01], axis=1))
        low_high, low_low = split(m11)
        top = dot(top_high, dy2) + dot(top_low, dy2)
        low = dot(low_high, dy2[half:]) + dot(low_low, dy2[half:])
        pieces.append((top, low))
    t_col[...] = sums
    dx[:half, at] = jnp.where(in_first, pieces[0][0], pieces[1][0])
    dx[half:, at] = jnp.where(in_first, pieces[0][1], pieces[1][1])


def plan(rows, bits, order):
    steps = []
    for bit in order:
        halves = rows % 16 == 0
        rows = rows // 2 if halves else rows
        steps.append((bit, rows, halves))
    return steps


def layer_kernel(
    bits, scenes, plans, chunk_rows, heads, width,
    tile, step, log_rate, gain, hidden_hbm, weight_hbm, x_hbm, dy_hbm,
    grad_x, grad_step, out, rate_out, skip_out,
    hidden, weight, x, dy, zs, tt, rt, back_all, dx, qt, g, l_row, l_col, r_row, t_col, w, small, acc, sacc, *rest
):
    bufs = rest[: len(plans)]
    sbuf, sems_send, sems_recv, sems_load = rest[len(plans) :]
    seq, dp = lax.axis_index("seq"), lax.axis_index("dp")
    first = seq == 0
    share = out.shape[0]
    tokens = x.shape[0]
    state = weight.shape[1] // 2
    slabs = x.shape[1] // SLAB

    def flipped(bit):
        mine = lax.rem(dp // (1 << bit), 2)
        return mine, dp + (1 - 2 * mine) * (1 << bit)

    other = 1 - seq
    loads = [
        pltpu.make_async_copy(src, dst, sems_load.at[n])
        for n, (src, dst) in enumerate(((hidden_hbm, hidden), (weight_hbm, weight), (x_hbm, x), (dy_hbm, dy)))
    ]
    for load in loads:
        load.start()
    barrier = pltpu.get_barrier_semaphore()
    pl.semaphore_signal(barrier, inc=1, device_id=(other, dp), device_id_type=MESH)
    for bit in range(bits):
        pl.semaphore_signal(barrier, inc=1, device_id=(seq, flipped(bit)[1]), device_id_type=MESH)

    count = [0]
    pending = []

    def send(src, dst, target):
        n = count[0]
        count[0] += 1
        copy = pltpu.make_async_remote_copy(
            src_ref=src, dst_ref=dst, send_sem=sems_send.at[n], recv_sem=sems_recv.at[n],
            device_id=target, device_id_type=MESH,
        )
        copy.start()
        pending.append(copy)
        return copy

    mask = jnp.where(tile[0, 0] == 0, 1.0, 0.0).astype(F32)
    on_first = jnp.where(first, 1.0, 0.0).astype(F32)
    rate = -jnp.exp(to_column(log_rate[...], heads))
    masked = step[...] * mask
    rows = lax.broadcasted_iota(jnp.int32, (tokens, tokens), 0)
    cols = lax.broadcasted_iota(jnp.int32, (tokens, tokens), 1)
    running = dot(masked * rate, jnp.where(rows <= cols, 1.0, 0.0).astype(F32), precision=EXACT)
    alpha = jnp.where(first, jnp.exp(running[:, tokens - 1 :] - running) * masked, jnp.exp(running) * mask)
    alpha_high, alpha_low = split(pad_rows(alpha).T)
    both_alpha = jnp.concatenate([alpha_high, alpha_low], axis=1)
    l_row[...] = running * LOG2E
    l_col[...] = pad_rows((running - jnp.log(step[...])) * LOG2E + (1.0 - mask) * 1e30).T

    loads[0].wait()
    loads[1].wait()
    projected = dot(hidden[...], weight[...])
    keys, query = projected[:, :state], projected[:, state:]
    both_keys = jnp.concatenate(split(jnp.where(first, keys, query)), axis=1)
    turned_keys = both_keys.T
    loads[2].wait()
    loads[3].wait()
    pl.semaphore_wait(barrier, bits + 1)
    swaps = []
    for n in range(slabs):
        at = slice(n * SLAB, (n + 1) * SLAB)
        spread = head_spread(n * SLAB, SLAB, width).astype(BF16)
        wide = dot(both_alpha, jnp.concatenate([spread, spread], axis=0))
        z = jnp.where(first, x[:, at].astype(F32), dy[:, at].astype(F32))
        scaled, scaled_low = split(z * wide)
        zs[:, at] = scaled
        both = dot(turned_keys, scaled) + dot(turned_keys, scaled_low)
        tt[n] = both[:state] + both[state:]
        swaps.append(send(tt.at[n], rt.at[n], (other, dp)))

    heads_part(heads, width, x, dy, l_row, l_col, qt)
    key_parts = jnp.concatenate(split(keys), axis=1)
    query_parts = jnp.concatenate(split(query), axis=1)
    q_high, q_low = split(qt[...])
    grad_b = dot(q_high, query_parts) + dot(q_low, query_parts)
    grad_c = dot(q_high, key_parts, ((0,), (0,))) + dot(q_low, key_parts, ((0,), (0,)))
    grad_keys = jnp.zeros((tokens, 2 * state), F32)
    for n in range(slabs):
        swaps[n].wait_recv()
        at = slice(n * SLAB, (n + 1) * SLAB)
        grad_keys += dot(zs[:, at], jnp.concatenate(split(rt[n]), axis=0), ((1,), (1,)))
    grad_b += on_first * grad_keys
    grad_c += (1.0 - on_first) * grad_keys
    grad_p = jnp.concatenate(
        [grad_b[:, :state] + grad_b[:, state:], grad_c[:, :state] + grad_c[:, state:]], axis=1
    ).astype(BF16)

    def aligned(v):
        return pl.multiple_of(v, 8)

    def weight_rows(start, rows):
        w[pl.ds(aligned(start), rows), :] = dot(
            hidden[:, pl.ds(pl.multiple_of(start, PAD), rows)], grad_p, ((0,), (0,))
        )

    chunks = range(len(plans))
    bases = [sum(chunk_rows[:c]) for c in range(len(plans))]
    copies = [None] * len(plans)
    for c in chunks:
        size = chunk_rows[c]
        weight_rows(other * share + bases[c], size)
        copies[c] = send(
            w.at[pl.ds(aligned(other * share + bases[c]), size)], bufs[c].at[pl.ds(0, size)], (other, dp)
        )

    pair_args = (heads, width, x, dy, l_row, l_col, g, dx, r_row, t_col)
    scale = 1.0 / scenes
    terms = {"carried": jnp.zeros((tokens, PAD), F32), "skip": jnp.zeros((8, PAD), F32)}
    light = [-1, None]

    def run_pairs(lo, hi):
        if lo == 0:
            g[...] = dot(keys, query, ((1,), (1,)), EXACT)
            t_col[...] = jnp.zeros_like(t_col)

        @pl.loop(lo, hi)
        def _(k):
            one_pair(k, *pair_args)

    def run_carried(n):
        at = slice(n * SLAB, (n + 1) * SLAB)
        spread = head_spread(n * SLAB, SLAB, width)
        spread_b = spread.astype(BF16)
        r_high, r_low = split(rt[n])
        back = dot(both_keys, jnp.concatenate([r_high, r_high], axis=0)) + dot(both_keys[:, :state], r_low)
        back_all[:, at] = back
        p_high, p_low = split(zs[:, at].astype(F32) * back)
        terms["carried"] += dot(p_high, spread_b, ((1,), (1,))) + dot(p_low, spread_b, ((1,), (1,)))
        total = jnp.sum(x[:, at].astype(F32) * dy[:, at].astype(F32), axis=0, keepdims=True)
        terms["skip"] += dot(jnp.broadcast_to(total, (8, SLAB)), spread, ((1,), (1,)), EXACT)

    def run_input(n):
        at = slice(n * SLAB, (n + 1) * SLAB)
        spread = head_spread(n * SLAB, SLAB, width)
        spread_b = spread.astype(BF16)
        gains = jnp.concatenate([gain[...] * mask, jnp.zeros((1, PAD - heads), F32)], axis=1)
        gain_row = dot(jnp.broadcast_to(gains, (8, PAD)), spread, precision=EXACT)[0:1]
        wide = dot(both_alpha, jnp.concatenate([spread_b, spread_b], axis=0)) * on_first
        grad_x[:, at] = (dx[:, at] + wide * back_all[:, at] + gain_row * dy[:, at].astype(F32)).astype(BF16)

    def run_last():
        crossing = terms["carried"].T[:heads]
        weighted = t_col[...].T[:heads]
        sign = 1.0 - 2.0 * on_first
        grad_l = r_row[...] - weighted + sign * crossing
        upper = jnp.where(rows >= cols, 1.0, 0.0).astype(F32)
        grad_log = dot(grad_l, upper, precision=EXACT)
        grad_log += on_first * jnp.sum(crossing, axis=1, keepdims=True)
        grad_step[...] = mask * ((weighted + on_first * crossing) / step[...] + rate * grad_log)
        grad_rate = jnp.sum(grad_log * masked, axis=1, keepdims=True) * rate
        row = lax.broadcasted_iota(jnp.int32, (8, PAD), 0)
        small[...] = jnp.where(row == 0, to_row(grad_rate, heads), jnp.where(row == 1, terms["skip"] * mask, 0.0))
        advance_small()

    def advance_small():
        stage = light[0]
        if stage > bits:
            return
        if stage >= 0:
            light[1].wait_recv()
            sacc[stage] = (small[...] if stage == 0 else sacc[stage - 1]) + sbuf[stage]
        light[0] = stage = stage + 1
        if stage == 0:
            light[1] = send(small, sbuf.at[0], (other, dp))
        elif stage <= bits:
            light[1] = send(sacc.at[stage - 1], sbuf.at[stage], (seq, flipped(stage - 1)[1]))

    quotas = list(QUOTAS)
    done = [0]
    pairs = heads // 2
    work = [functools.partial(run_carried, n) for n in range(slabs)] + [run_last]
    work += [functools.partial(run_input, n) for n in range(slabs)]

    def tick():
        n = quotas.pop(0) if quotas else 1
        if light[0] >= 0:
            advance_small()
        end = min(done[0] + n, pairs + len(work))
        if done[0] < min(end, pairs):
            run_pairs(done[0], min(end, pairs))
        for unit in range(max(done[0], pairs), end):
            work[unit - pairs]()
        done[0] = max(end, done[0])

    starts = list(bases)
    offsets = list(chunk_rows)
    history = [[] for _ in plans]

    def start_step(c, s):
        bit, kept, halves = plans[c][s]
        side, peer = flipped(bit)
        begin = starts[c]
        source = begin
        if halves:
            source = aligned(begin + (1 - side) * kept)
            starts[c] = aligned(begin + side * kept)
        offset = offsets[c]
        offsets[c] = offset + kept
        history[c].append((bit, kept, halves, starts[c]))
        copies[c] = send(acc.at[pl.ds(source, kept)], bufs[c].at[pl.ds(offset, kept)], (seq, peer))

    for c in chunks:
        weight_rows(seq * share + bases[c], chunk_rows[c])
    tick()
    for c in chunks:
        rows_here = chunk_rows[c]
        copies[c].wait_recv()
        mine = w[pl.ds(aligned(seq * share + bases[c]), rows_here), :]
        acc[pl.ds(bases[c], rows_here), :] = mine + bufs[c][0:rows_here, :]
        start_step(c, 0)

    for s in range(bits):
        for c in chunks:
            tick()
            kept, halves = plans[c][s][1:]
            copies[c].wait_recv()
            if not halves:
                copies[c].wait_send()
                pending[:] = [p for p in pending if p is not copies[c]]
            here = pl.ds(starts[c], kept)
            acc[here, :] = acc[here, :] + bufs[c][offsets[c] - kept : offsets[c], :]
            if s + 1 < bits:
                start_step(c, s + 1)
            else:
                out[here, :] = acc[here, :] * scale

    trail = [[h for h in reversed(history[c]) if h[2]] for c in range(len(plans))]

    def gather(c, n):
        bit, kept, _, start = trail[c][n]
        region = out.at[pl.ds(start, kept)]
        return send(region, region, (seq, flipped(bit)[1]))

    for c in chunks:
        copies[c] = gather(c, 0)
    for n in range(max(len(t) for t in trail)):
        for c in chunks:
            if n < len(trail[c]):
                tick()
                copies[c].wait_recv()
                if n + 1 < len(trail[c]):
                    copies[c] = gather(c, n + 1)
    while light[0] <= bits or done[0] < pairs + len(work):
        tick()
    total = sacc[bits] * scale
    total = jnp.where(seq == 0, total, pltpu.roll(total, PAD - heads // 2, 1))
    rate_out[...] = total[0:1, : heads // 2]
    skip_out[...] = total[1:2, : heads // 2]
    for copy in pending:
        copy.wait_send()


def emit_kernel(*refs):
    count = len(refs) // 2
    copies = [pltpu.make_async_copy(refs[n], refs[count + n], refs[-1].at[n]) for n in range(count)]
    for copy in copies:
        copy.start()
    for copy in copies:
        copy.wait()


def chunk_orders(bits):
    if bits < 4:
        return [list(range(bits))] * 3
    late = list(range(3, bits))
    return [0, 2, 1] + late, [1, 0, 2] + late, [2, 1, 0] + late


def shards(hidden, scan_input, grad_out, step_size, proj_weight, log_rate, skip_gain, tile_list):
    tokens, inner = scan_input.shape[1:]
    model, two_state = proj_weight.shape
    heads = log_rate.shape[0]
    width = inner // heads
    slabs, state = inner // SLAB, two_state // 2
    scenes, seqs = lax.axis_size("dp"), lax.axis_size("seq")
    bits = scenes.bit_length() - 1
    rows = model // seqs
    low = rows // (3 * PAD) * PAD
    chunk_rows = (low, low, rows - 2 * low)
    plans = [plan(r, bits, o) for r, o in zip(chunk_rows, chunk_orders(bits))]

    def shape(*dims, dtype=F32):
        return jax.ShapeDtypeStruct(dims, dtype)

    scratch = [
        pltpu.VMEM((tokens, model), BF16), pltpu.VMEM((model, two_state), BF16),
        pltpu.VMEM((tokens, inner), BF16), pltpu.VMEM((tokens, inner), BF16), pltpu.VMEM((tokens, inner), BF16),
        pltpu.VMEM((slabs, state, SLAB), F32), pltpu.VMEM((slabs, state, SLAB), F32),
        pltpu.VMEM((tokens, inner), F32), pltpu.VMEM((tokens, inner), F32),
        pltpu.VMEM((tokens, tokens), F32), pltpu.VMEM((tokens, tokens), F32),
        pltpu.VMEM((heads, tokens), F32), pltpu.VMEM((tokens, PAD), F32),
        pltpu.VMEM((heads, tokens), F32), pltpu.VMEM((tokens, PAD), F32),
        pltpu.VMEM((model, two_state), F32), pltpu.VMEM((8, PAD), F32),
        pltpu.VMEM((rows, two_state), F32), pltpu.VMEM((bits + 1, 8, PAD), F32),
    ]
    for r, steps in zip(chunk_rows, plans):
        scratch.append(pltpu.VMEM((r + sum(k for _, k, _ in steps), two_state), F32))
    scratch.append(pltpu.VMEM((bits + 1, 8, PAD), F32))
    copies = slabs + len(plans) * (1 + 2 * bits) + bits + 1
    scratch += [pltpu.SemaphoreType.DMA((copies,)), pltpu.SemaphoreType.DMA((copies,)), pltpu.SemaphoreType.DMA((4,))]
    anywhere = pl.BlockSpec(memory_space=pl.ANY)
    out_shape = (
        shape(tokens, inner, dtype=BF16), shape(heads, tokens), shape(rows, two_state),
        shape(1, heads // seqs), shape(1, heads // seqs),
    )
    outs = pl.pallas_call(
        functools.partial(layer_kernel, bits, scenes, plans, chunk_rows, heads, width),
        out_shape=out_shape,
        in_specs=[SMEM] + [VMEM] * 3 + [anywhere] * 4,
        out_specs=(VMEM,) * 5,
        scratch_shapes=scratch,
        compiler_params=pltpu.CompilerParams(
            collective_id=0, has_side_effects=True, vmem_limit_bytes=48 * 1024 * 1024
        ),
        name="layer",
    )(
        tile_list, step_size[0], log_rate[None], skip_gain[None],
        hidden[0], proj_weight, scan_input[0], grad_out[0],
    )
    grad_x, grad_step, summed, rates, gains = pl.pallas_call(
        emit_kernel,
        out_shape=out_shape,
        in_specs=[anywhere] * 5,
        out_specs=(anywhere,) * 5,
        scratch_shapes=[pltpu.SemaphoreType.DMA((5,))],
        name="emit",
    )(*outs)
    return grad_x[None], grad_step[None], summed, rates[0], gains[0]


def solution(mesh):
    in_specs = (
        P("dp", "seq", None),
        P("dp", "seq", None),
        P("dp", "seq", None),
        P("dp", None, "seq"),
        P(),
        P(),
        P(),
        P("dp", "seq"),
    )
    out_specs = (P("dp", "seq", None), P("dp", None, "seq"), P("seq", None), P("seq"), P("seq"))
    return jax.shard_map(shards, mesh=mesh, in_specs=in_specs, out_specs=out_specs, check_vma=False)
```

```python
import functools

import jax
import jax.numpy as jnp
from jax import lax
from jax.experimental import pallas as pl
from jax.experimental.pallas import tpu as pltpu
from jax.sharding import PartitionSpec as P

MESH = pl.DeviceIdType.MESH
EXACT = lax.Precision.HIGHEST
F32 = jnp.float32
BF16 = jnp.bfloat16
LOG2E = 1.4426950408889634
PAD = 128
SLAB = 512
QUOTAS = (2, 6, 0, 0, 4, 0, 0, 2, 2, 0, 4, 1, 0, 2, 1, 0, 1, 1, 0, 1, 1, 0, 1, 1, 1)
VMEM = pl.BlockSpec(memory_space=pltpu.VMEM)
SMEM = pl.BlockSpec(memory_space=pltpu.SMEM)


def dot(a, b, dims=((1,), (0,)), precision=None):
    return lax.dot_general(a, b, (dims, ((), ())), precision=precision, preferred_element_type=F32)


def split(a):
    high = a.astype(BF16)
    return high, (a - high.astype(F32)).astype(BF16)


def to_column(row, count):
    rows = lax.broadcasted_iota(jnp.int32, (count, count), 0)
    cols = lax.broadcasted_iota(jnp.int32, (count, count), 1)
    return jnp.sum(jnp.where(rows == cols, row, 0.0), axis=1, keepdims=True)


def to_row(column, count):
    rows = lax.broadcasted_iota(jnp.int32, (count, PAD), 0)
    cols = lax.broadcasted_iota(jnp.int32, (count, PAD), 1)
    return jnp.sum(jnp.where(rows == cols, column, 0.0), axis=0, keepdims=True)


def head_spread(start, size, width):
    rows = lax.broadcasted_iota(jnp.int32, (PAD, size), 0)
    cols = lax.broadcasted_iota(jnp.int32, (PAD, size), 1) + start
    return jnp.where((cols >= rows * width) & (cols < (rows + 1) * width), 1.0, 0.0).astype(F32)


def pad_rows(a):
    return jnp.concatenate([a, jnp.zeros((PAD - a.shape[0], a.shape[1]), a.dtype)], axis=0)


def pair_parts(k, turned, lane, width, x, dy, l_row):
    tokens = x.shape[0]
    half = tokens // 2
    pair = 2 * width
    rows = lax.broadcasted_iota(jnp.int32, (half, half), 0)
    cols = lax.broadcasted_iota(jnp.int32, (half, half), 1)
    causal = cols >= rows
    in_first = lax.broadcasted_iota(jnp.int32, (1, pair), 1) < width
    keep = [jnp.where(in_first, 1.0, 0.0).astype(BF16), jnp.where(in_first, 0.0, 1.0).astype(BF16)]
    at = pl.ds(pl.multiple_of(k * pair, pair), pair)
    x2 = x[:, at]
    dy2 = dy[:, at]
    sides = []
    for side in range(2):
        l_j = turned[:, lane + side : lane + side + 1]
        l_i = l_row[pl.ds(2 * k + side, 1), :]
        xs = x2 * keep[side]
        w_top = dot(xs[:half], dy2, ((1,), (1,)))
        w_low = dot(xs[half:], dy2[half:], ((1,), (1,)))
        d00 = jnp.exp2(jnp.where(causal, l_i[:, :half] - l_j[:half], -1e30))
        d01 = jnp.exp2(l_i[:, half:] - l_j[:half])
        d11 = jnp.exp2(jnp.where(causal, l_i[:, half:] - l_j[half:], -1e30))
        sides.append(((d00, w_top[:, :half]), (d01, w_top[:, half:]), (d11, w_low)))
    return at, dy2, in_first, sides


def turn(l_col, k):
    return pltpu.roll(l_col[...], lax.rem(PAD - 2 * k, PAD), 1)


def heads_part(heads, width, x, dy, l_row, l_col, qt):
    half = x.shape[0] // 2
    qt[...] = jnp.zeros_like(qt)
    group = 4 if heads % 8 == 0 else 1

    @pl.loop(0, heads // 2 // group)
    def _(step):
        turned = turn(l_col, step * group)
        parts = []
        for n in range(group):
            parts += pair_parts(step * group + n, turned, 2 * n, width, x, dy, l_row)[3]
        for n, (j, i) in enumerate(((0, 0), (0, 1), (1, 1))):
            js, at_i = slice(j * half, (j + 1) * half), slice(i * half, (i + 1) * half)
            qt[js, at_i] += sum(side[n][0] * side[n][1] for side in parts)


def one_pair(k, turned, lane, width, x, dy, l_row, g, dx, r_row, t_col):
    tokens = x.shape[0]
    half = tokens // 2
    lanes = lax.broadcasted_iota(jnp.int32, (tokens, PAD), 1)
    at, dy2, in_first, sides = pair_parts(k, turned, lane, width, x, dy, l_row)
    sums = t_col[...]
    pieces = []
    for side in range(2):
        head = 2 * k + side
        (d00, w00), (d01, w01), (d11, w11) = sides[side]
        m00, m01, m11 = d00 * g[:half, :half], d01 * g[:half, half:], d11 * g[half:, half:]
        e00, e01, e11 = m00 * w00, m01 * w01, m11 * w11
        r_row[pl.ds(head, 1), :] = jnp.concatenate(
            [jnp.sum(e00, axis=0, keepdims=True), jnp.sum(e01 + e11, axis=0, keepdims=True)], axis=1
        )
        column = jnp.concatenate(
            [jnp.sum(e00 + e01, axis=1, keepdims=True), jnp.sum(e11, axis=1, keepdims=True)], axis=0
        )
        sums = jnp.where(lanes == head, column, sums)
        top_high, top_low = split(jnp.concatenate([m00, m01], axis=1))
        low_high, low_low = split(m11)
        top = dot(top_high, dy2) + dot(top_low, dy2)
        low = dot(low_high, dy2[half:]) + dot(low_low, dy2[half:])
        pieces.append((top, low))
    t_col[...] = sums
    dx[:half, at] = jnp.where(in_first, pieces[0][0], pieces[1][0])
    dx[half:, at] = jnp.where(in_first, pieces[0][1], pieces[1][1])


def plan(rows, bits, order):
    steps = []
    for bit in order:
        halves = rows % 16 == 0
        rows = rows // 2 if halves else rows
        steps.append((bit, rows, halves))
    return steps


def layer_kernel(
    bits, scenes, plans, chunk_rows, heads, width,
    tile, step_hbm, rate_hbm, gain_hbm, hidden_hbm, weight_hbm, x_hbm, dy_hbm,
    grad_x, grad_step, out, rate_out, skip_out,
    step, log_rate, gain, hidden, weight, x, dy, spread_all, zs, tt, rt, back_all, dx, qt, g, l_row, l_col, r_row, t_col, w, small, acc, sacc, *rest
):
    bufs = rest[: len(plans)]
    sbuf, sems_send, sems_recv, sems_load = rest[len(plans) :]
    seq, dp = lax.axis_index("seq"), lax.axis_index("dp")
    first = seq == 0
    share = out.shape[0]
    tokens = x.shape[0]
    state = weight.shape[1] // 2
    slabs = x.shape[1] // SLAB

    def flipped(bit):
        mine = lax.rem(dp // (1 << bit), 2)
        return mine, dp + (1 - 2 * mine) * (1 << bit)

    other = 1 - seq
    loads = [
        pltpu.make_async_copy(src, dst, sems_load.at[n])
        for n, (src, dst) in enumerate((
            (step_hbm, step), (rate_hbm, log_rate), (gain_hbm, gain),
            (hidden_hbm, hidden), (weight_hbm, weight), (x_hbm, x), (dy_hbm, dy),
        ))
    ]
    for load in loads:
        load.start()
    barrier = pltpu.get_barrier_semaphore()
    pl.semaphore_signal(barrier, inc=1, device_id=(other, dp), device_id_type=MESH)
    for bit in range(bits):
        pl.semaphore_signal(barrier, inc=1, device_id=(seq, flipped(bit)[1]), device_id_type=MESH)

    count = [0]
    pending = []

    def send(src, dst, target):
        n = count[0]
        count[0] += 1
        copy = pltpu.make_async_remote_copy(
            src_ref=src, dst_ref=dst, send_sem=sems_send.at[n], recv_sem=sems_recv.at[n],
            device_id=target, device_id_type=MESH,
        )
        copy.start()
        pending.append(copy)
        return copy

    for n in range(slabs):
        spread_all[:, n * SLAB : (n + 1) * SLAB] = head_spread(n * SLAB, SLAB, width).astype(BF16)
    for load in loads[:3]:
        load.wait()
    mask = jnp.where(tile[0, 0] == 0, 1.0, 0.0).astype(F32)
    on_first = jnp.where(first, 1.0, 0.0).astype(F32)
    rate = -jnp.exp(to_column(log_rate[...], heads))
    masked = step[...] * mask
    rows = lax.broadcasted_iota(jnp.int32, (tokens, tokens), 0)
    cols = lax.broadcasted_iota(jnp.int32, (tokens, tokens), 1)
    running = dot(masked * rate, jnp.where(rows <= cols, 1.0, 0.0).astype(F32), precision=EXACT)
    alpha = jnp.where(first, jnp.exp(running[:, tokens - 1 :] - running) * masked, jnp.exp(running) * mask)
    alpha_high, alpha_low = split(pad_rows(alpha).T)
    both_alpha = jnp.concatenate([alpha_high, alpha_low], axis=1)
    gains = jnp.concatenate([gain[...] * mask, jnp.zeros((1, PAD - heads), F32)], axis=1)
    gain_parts = jnp.concatenate(split(jnp.broadcast_to(gains, (16, PAD))), axis=1)
    l_row[...] = running * LOG2E
    l_col[...] = pad_rows((running - jnp.log(step[...])) * LOG2E + (1.0 - mask) * 1e30).T

    loads[3].wait()
    loads[4].wait()
    projected = dot(hidden[...], weight[...])
    keys, query = projected[:, :state], projected[:, state:]
    both_keys = jnp.concatenate(split(jnp.where(first, keys, query)), axis=1)
    turned_keys = both_keys.T
    loads[5].wait()
    loads[6].wait()
    pl.semaphore_wait(barrier, bits + 1)
    swaps = []
    for n in range(slabs):
        at = slice(n * SLAB, (n + 1) * SLAB)
        spread = spread_all[:, at]
        wide = dot(both_alpha, jnp.concatenate([spread, spread], axis=0))
        z = jnp.where(first, x[:, at].astype(F32), dy[:, at].astype(F32))
        scaled, scaled_low = split(z * wide)
        zs[:, at] = scaled
        both = dot(turned_keys, scaled) + dot(turned_keys, scaled_low)
        tt[n] = both[:state] + both[state:]
        swaps.append(send(tt.at[n], rt.at[n], (other, dp)))

    heads_part(heads, width, x, dy, l_row, l_col, qt)
    key_parts = jnp.concatenate(split(keys), axis=1)
    query_parts = jnp.concatenate(split(query), axis=1)
    q_high, q_low = split(qt[...])
    grad_b = dot(q_high, query_parts) + dot(q_low, query_parts)
    grad_c = dot(q_high, key_parts, ((0,), (0,))) + dot(q_low, key_parts, ((0,), (0,)))
    grad_keys = jnp.zeros((tokens, 2 * state), F32)
    for n in range(slabs):
        swaps[n].wait_recv()
        at = slice(n * SLAB, (n + 1) * SLAB)
        grad_keys += dot(zs[:, at], jnp.concatenate(split(rt[n]), axis=0), ((1,), (1,)))
    grad_b += on_first * grad_keys
    grad_c += (1.0 - on_first) * grad_keys
    grad_p = jnp.concatenate(
        [grad_b[:, :state] + grad_b[:, state:], grad_c[:, :state] + grad_c[:, state:]], axis=1
    ).astype(BF16)

    def aligned(v):
        return pl.multiple_of(v, 8)

    def weight_rows(start, rows):
        w[pl.ds(aligned(start), rows), :] = dot(
            hidden[:, pl.ds(pl.multiple_of(start, PAD), rows)], grad_p, ((0,), (0,))
        )

    chunks = range(len(plans))
    bases = [sum(chunk_rows[:c]) for c in range(len(plans))]
    copies = [None] * len(plans)
    for c in chunks:
        size = chunk_rows[c]
        weight_rows(other * share + bases[c], size)
        copies[c] = send(
            w.at[pl.ds(aligned(other * share + bases[c]), size)], bufs[c].at[pl.ds(0, size)], (other, dp)
        )

    pair_args = (width, x, dy, l_row, g, dx, r_row, t_col)
    scale = 1.0 / scenes
    terms = {"carried": jnp.zeros((tokens, PAD), F32), "skip": jnp.zeros((8, PAD), F32)}
    light = [-1, None]

    def run_pairs(lo, hi):
        if lo == 0:
            g[...] = dot(keys, query, ((1,), (1,)), EXACT)
            t_col[...] = jnp.zeros_like(t_col)

        if hi - lo > 1:

            @pl.loop(0, (hi - lo) // 2)
            def _(n):
                turned = turn(l_col, lo + 2 * n)
                one_pair(lo + 2 * n, turned, 0, *pair_args)
                one_pair(lo + 2 * n + 1, turned, 2, *pair_args)

        if (hi - lo) % 2:
            one_pair(hi - 1, turn(l_col, hi - 1), 0, *pair_args)

    def run_carried(n):
        at = slice(n * SLAB, (n + 1) * SLAB)
        spread = spread_all[:, at]
        r_high, r_low = split(rt[n])
        back = dot(both_keys, jnp.concatenate([r_high, r_high], axis=0)) + dot(both_keys[:, :state], r_low)
        back_all[:, at] = back
        p_high, p_low = split(zs[:, at].astype(F32) * back)
        total = jnp.sum(x[:, at].astype(F32) * dy[:, at].astype(F32), axis=0, keepdims=True)
        t_high, t_low = split(jnp.broadcast_to(total, (16, SLAB)))
        summed = dot(jnp.concatenate([p_high, p_low, t_high, t_low], axis=0), spread, ((1,), (1,)))
        terms["carried"] += summed[:tokens] + summed[tokens : 2 * tokens]
        terms["skip"] += summed[2 * tokens : 2 * tokens + 8] + summed[2 * tokens + 16 : 2 * tokens + 24]

    def run_input(n):
        at = slice(n * SLAB, (n + 1) * SLAB)
        spread = spread_all[:, at]
        both = dot(
            jnp.concatenate([both_alpha, gain_parts], axis=0), jnp.concatenate([spread, spread], axis=0)
        )
        wide, gain_row = both[:tokens] * on_first, both[tokens : tokens + 1]
        grad_x[:, at] = (dx[:, at] + wide * back_all[:, at] + gain_row * dy[:, at].astype(F32)).astype(BF16)

    def run_last():
        crossing = terms["carried"].T[:heads]
        weighted = t_col[...].T[:heads]
        sign = 1.0 - 2.0 * on_first
        grad_l = r_row[...] - weighted + sign * crossing
        upper = jnp.where(rows >= cols, 1.0, 0.0).astype(F32)
        grad_log = dot(grad_l, upper, precision=EXACT)
        grad_log += on_first * jnp.sum(crossing, axis=1, keepdims=True)
        grad_step[...] = mask * ((weighted + on_first * crossing) / step[...] + rate * grad_log)
        grad_rate = jnp.sum(grad_log * masked, axis=1, keepdims=True) * rate
        row = lax.broadcasted_iota(jnp.int32, (8, PAD), 0)
        small[...] = jnp.where(row == 0, to_row(grad_rate, heads), jnp.where(row == 1, terms["skip"] * mask, 0.0))
        advance_small()

    def advance_small():
        stage = light[0]
        if stage > bits:
            return
        if stage >= 0:
            light[1].wait_recv()
            sacc[stage] = (small[...] if stage == 0 else sacc[stage - 1]) + sbuf[stage]
        light[0] = stage = stage + 1
        if stage == 0:
            light[1] = send(small, sbuf.at[0], (other, dp))
        elif stage <= bits:
            light[1] = send(sacc.at[stage - 1], sbuf.at[stage], (seq, flipped(stage - 1)[1]))

    quotas = list(QUOTAS)
    done = [0]
    pairs = heads // 2
    work = [functools.partial(run_carried, n) for n in range(slabs)] + [run_last]
    work += [functools.partial(run_input, n) for n in range(slabs)]

    def tick():
        n = quotas.pop(0) if quotas else 1
        if light[0] >= 0:
            advance_small()
        end = min(done[0] + n, pairs + len(work))
        if done[0] < min(end, pairs):
            run_pairs(done[0], min(end, pairs))
        for unit in range(max(done[0], pairs), end):
            work[unit - pairs]()
        done[0] = max(end, done[0])

    starts = list(bases)
    offsets = list(chunk_rows)
    history = [[] for _ in plans]

    def start_step(c, s):
        bit, kept, halves = plans[c][s]
        side, peer = flipped(bit)
        begin = starts[c]
        source = begin
        if halves:
            source = aligned(begin + (1 - side) * kept)
            starts[c] = aligned(begin + side * kept)
        offset = offsets[c]
        offsets[c] = offset + kept
        history[c].append((bit, kept, halves, starts[c]))
        copies[c] = send(acc.at[pl.ds(source, kept)], bufs[c].at[pl.ds(offset, kept)], (seq, peer))

    for c in chunks:
        weight_rows(seq * share + bases[c], chunk_rows[c])
    tick()
    for c in chunks:
        rows_here = chunk_rows[c]
        copies[c].wait_recv()
        mine = w[pl.ds(aligned(seq * share + bases[c]), rows_here), :]
        acc[pl.ds(bases[c], rows_here), :] = mine + bufs[c][0:rows_here, :]
        start_step(c, 0)

    for s in range(bits):
        for c in chunks:
            tick()
            kept, halves = plans[c][s][1:]
            copies[c].wait_recv()
            if not halves:
                copies[c].wait_send()
                pending[:] = [p for p in pending if p is not copies[c]]
            here = pl.ds(starts[c], kept)
            acc[here, :] = acc[here, :] + bufs[c][offsets[c] - kept : offsets[c], :]
            if s + 1 < bits:
                start_step(c, s + 1)
            else:
                out[here, :] = acc[here, :] * scale

    trail = [[h for h in reversed(history[c]) if h[2]] for c in range(len(plans))]

    def gather(c, n):
        bit, kept, _, start = trail[c][n]
        region = out.at[pl.ds(start, kept)]
        return send(region, region, (seq, flipped(bit)[1]))

    for c in chunks:
        copies[c] = gather(c, 0)
    for n in range(max(len(t) for t in trail)):
        for c in chunks:
            if n < len(trail[c]):
                tick()
                copies[c].wait_recv()
                if n + 1 < len(trail[c]):
                    copies[c] = gather(c, n + 1)
    while light[0] <= bits or done[0] < pairs + len(work):
        tick()
    total = sacc[bits] * scale
    total = jnp.where(seq == 0, total, pltpu.roll(total, PAD - heads // 2, 1))
    rate_out[...] = total[0:1, : heads // 2]
    skip_out[...] = total[1:2, : heads // 2]
    for copy in pending:
        copy.wait_send()


def emit_kernel(*refs):
    count = len(refs) // 2
    for n in range(count):
        refs[count + n][...] = refs[n][...]


def chunk_orders(bits):
    if bits < 4:
        return [list(range(bits))] * 3
    late = list(range(3, bits))
    return [0, 2, 1] + late, [1, 0, 2] + late, [2, 1, 0] + late


def shards(hidden, scan_input, grad_out, step_size, proj_weight, log_rate, skip_gain, tile_list):
    tokens, inner = scan_input.shape[1:]
    model, two_state = proj_weight.shape
    heads = log_rate.shape[0]
    width = inner // heads
    slabs, state = inner // SLAB, two_state // 2
    scenes, seqs = lax.axis_size("dp"), lax.axis_size("seq")
    bits = scenes.bit_length() - 1
    rows = model // seqs
    low = rows // (3 * PAD) * PAD
    chunk_rows = (low, low, rows - 2 * low)
    plans = [plan(r, bits, o) for r, o in zip(chunk_rows, chunk_orders(bits))]

    def shape(*dims, dtype=F32):
        return jax.ShapeDtypeStruct(dims, dtype)

    scratch = [
        pltpu.VMEM((heads, tokens), F32), pltpu.VMEM((1, heads), F32), pltpu.VMEM((1, heads), F32),
        pltpu.VMEM((tokens, model), BF16), pltpu.VMEM((model, two_state), BF16),
        pltpu.VMEM((tokens, inner), BF16), pltpu.VMEM((tokens, inner), BF16),
        pltpu.VMEM((PAD, inner), BF16), pltpu.VMEM((tokens, inner), BF16),
        pltpu.VMEM((slabs, state, SLAB), F32), pltpu.VMEM((slabs, state, SLAB), F32),
        pltpu.VMEM((tokens, inner), F32), pltpu.VMEM((tokens, inner), F32),
        pltpu.VMEM((tokens, tokens), F32), pltpu.VMEM((tokens, tokens), F32),
        pltpu.VMEM((heads, tokens), F32), pltpu.VMEM((tokens, PAD), F32),
        pltpu.VMEM((heads, tokens), F32), pltpu.VMEM((tokens, PAD), F32),
        pltpu.VMEM((model, two_state), F32), pltpu.VMEM((8, PAD), F32),
        pltpu.VMEM((rows, two_state), F32), pltpu.VMEM((bits + 1, 8, PAD), F32),
    ]
    for r, steps in zip(chunk_rows, plans):
        scratch.append(pltpu.VMEM((r + sum(k for _, k, _ in steps), two_state), F32))
    scratch.append(pltpu.VMEM((bits + 1, 8, PAD), F32))
    copies = slabs + len(plans) * (1 + 2 * bits) + bits + 1
    scratch += [pltpu.SemaphoreType.DMA((copies,)), pltpu.SemaphoreType.DMA((copies,)), pltpu.SemaphoreType.DMA((7,))]
    stored = pl.BlockSpec(memory_space=pltpu.HBM)
    out_shape = (
        shape(tokens, inner, dtype=BF16), shape(heads, tokens), shape(rows, two_state),
        shape(1, heads // seqs), shape(1, heads // seqs),
    )
    outs = pl.pallas_call(
        functools.partial(layer_kernel, bits, scenes, plans, chunk_rows, heads, width),
        out_shape=out_shape,
        in_specs=[SMEM] + [stored] * 7,
        out_specs=(VMEM,) * 5,
        scratch_shapes=scratch,
        compiler_params=pltpu.CompilerParams(
            collective_id=0, has_side_effects=True, vmem_limit_bytes=48 * 1024 * 1024
        ),
        name="layer",
    )(
        tile_list, step_size[0], log_rate[None], skip_gain[None],
        hidden[0], proj_weight, scan_input[0], grad_out[0],
    )
    grad_x, grad_step, summed, rates, gains = pl.pallas_call(
        emit_kernel,
        out_shape=out_shape,
        in_specs=[VMEM] * 5,
        out_specs=(VMEM,) * 5,
        name="emit",
    )(*outs)
    return grad_x[None], grad_step[None], summed, rates[0], gains[0]


def solution(mesh):
    in_specs = (
        P("dp", "seq", None),
        P("dp", "seq", None),
        P("dp", "seq", None),
        P("dp", None, "seq"),
        P(),
        P(),
        P(),
        P("dp", "seq"),
    )
    out_specs = (P("dp", "seq", None), P("dp", None, "seq"), P("seq", None), P("seq"), P("seq"))
    return jax.shard_map(shards, mesh=mesh, in_specs=in_specs, out_specs=out_specs, check_vma=False)
```

```python
import functools

import jax
import jax.numpy as jnp
from jax import lax
from jax.experimental import pallas as pl
from jax.experimental.pallas import tpu as pltpu
from jax.sharding import PartitionSpec as P

MESH = pl.DeviceIdType.MESH
EXACT = lax.Precision.HIGHEST
F32 = jnp.float32
BF16 = jnp.bfloat16
LOG2E = 1.4426950408889634
PAD = 128
SLAB = 512
QUOTAS = (2, 6, 0, 0, 4, 0, 0, 2, 2, 0, 4, 1, 0, 2, 1, 0, 1, 1, 0, 1, 1, 0, 1, 1, 1)
VMEM = pl.BlockSpec(memory_space=pltpu.VMEM)
SMEM = pl.BlockSpec(memory_space=pltpu.SMEM)


def dot(a, b, dims=((1,), (0,)), precision=None):
    return lax.dot_general(a, b, (dims, ((), ())), precision=precision, preferred_element_type=F32)


def split(a):
    high = a.astype(BF16)
    return high, (a - high.astype(F32)).astype(BF16)


def to_column(row, count):
    rows = lax.broadcasted_iota(jnp.int32, (count, count), 0)
    cols = lax.broadcasted_iota(jnp.int32, (count, count), 1)
    return jnp.sum(jnp.where(rows == cols, row, 0.0), axis=1, keepdims=True)


def to_row(column, count):
    rows = lax.broadcasted_iota(jnp.int32, (count, PAD), 0)
    cols = lax.broadcasted_iota(jnp.int32, (count, PAD), 1)
    return jnp.sum(jnp.where(rows == cols, column, 0.0), axis=0, keepdims=True)


def head_spread(start, size, width):
    rows = lax.broadcasted_iota(jnp.int32, (PAD, size), 0)
    cols = lax.broadcasted_iota(jnp.int32, (PAD, size), 1) + start
    return jnp.where((cols >= rows * width) & (cols < (rows + 1) * width), 1.0, 0.0).astype(F32)


def pad_rows(a):
    return jnp.concatenate([a, jnp.zeros((PAD - a.shape[0], a.shape[1]), a.dtype)], axis=0)


def pair_parts(k, turned, lane, width, x, dy, l_row):
    tokens = x.shape[0]
    half = tokens // 2
    pair = 2 * width
    rows = lax.broadcasted_iota(jnp.int32, (half, half), 0)
    cols = lax.broadcasted_iota(jnp.int32, (half, half), 1)
    causal = cols >= rows
    in_first = lax.broadcasted_iota(jnp.int32, (1, pair), 1) < width
    keep = [jnp.where(in_first, 1.0, 0.0).astype(BF16), jnp.where(in_first, 0.0, 1.0).astype(BF16)]
    at = pl.ds(pl.multiple_of(k * pair, pair), pair)
    x2 = x[:, at]
    dy2 = dy[:, at]
    sides = []
    for side in range(2):
        l_j = turned[:, lane + side : lane + side + 1]
        l_i = l_row[pl.ds(2 * k + side, 1), :]
        xs = x2 * keep[side]
        w_top = dot(xs[:half], dy2, ((1,), (1,)))
        w_low = dot(xs[half:], dy2[half:], ((1,), (1,)))
        d00 = jnp.exp2(jnp.where(causal, l_i[:, :half] - l_j[:half], -1e30))
        d01 = jnp.exp2(l_i[:, half:] - l_j[:half])
        d11 = jnp.exp2(jnp.where(causal, l_i[:, half:] - l_j[half:], -1e30))
        sides.append(((d00, w_top[:, :half]), (d01, w_top[:, half:]), (d11, w_low)))
    return at, dy2, in_first, sides


def turn(l_col, k):
    return pltpu.roll(l_col[...], lax.rem(PAD - 2 * k, PAD), 1)


def heads_part(heads, width, x, dy, l_row, l_col, qt):
    half = x.shape[0] // 2
    qt[...] = jnp.zeros_like(qt)
    group = 4 if heads % 8 == 0 else 1

    @pl.loop(0, heads // 2 // group)
    def _(step):
        turned = turn(l_col, step * group)
        parts = []
        for n in range(group):
            parts += pair_parts(step * group + n, turned, 2 * n, width, x, dy, l_row)[3]
        for n, (j, i) in enumerate(((0, 0), (0, 1), (1, 1))):
            js, at_i = slice(j * half, (j + 1) * half), slice(i * half, (i + 1) * half)
            qt[js, at_i] += sum(side[n][0] * side[n][1] for side in parts)


def one_pair(k, turned, lane, width, x, dy, l_row, g, dx, r_row, t_col):
    tokens = x.shape[0]
    half = tokens // 2
    lanes = lax.broadcasted_iota(jnp.int32, (tokens, PAD), 1)
    at, dy2, in_first, sides = pair_parts(k, turned, lane, width, x, dy, l_row)
    sums = t_col[...]
    pieces = []
    for side in range(2):
        head = 2 * k + side
        (d00, w00), (d01, w01), (d11, w11) = sides[side]
        m00, m01, m11 = d00 * g[:half, :half], d01 * g[:half, half:], d11 * g[half:, half:]
        e00, e01, e11 = m00 * w00, m01 * w01, m11 * w11
        r_row[pl.ds(head, 1), :] = jnp.concatenate(
            [jnp.sum(e00, axis=0, keepdims=True), jnp.sum(e01 + e11, axis=0, keepdims=True)], axis=1
        )
        column = jnp.concatenate(
            [jnp.sum(e00 + e01, axis=1, keepdims=True), jnp.sum(e11, axis=1, keepdims=True)], axis=0
        )
        sums = jnp.where(lanes == head, column, sums)
        top_high, top_low = split(jnp.concatenate([m00, m01], axis=1))
        low_high, low_low = split(m11)
        top = dot(top_high, dy2) + dot(top_low, dy2)
        low = dot(low_high, dy2[half:]) + dot(low_low, dy2[half:])
        pieces.append((top, low))
    t_col[...] = sums
    dx[:half, at] = jnp.where(in_first, pieces[0][0], pieces[1][0])
    dx[half:, at] = jnp.where(in_first, pieces[0][1], pieces[1][1])


def plan(rows, bits, order):
    steps = []
    for bit in order:
        halves = rows % 16 == 0
        rows = rows // 2 if halves else rows
        steps.append((bit, rows, halves))
    return steps


def layer_kernel(
    bits, scenes, plans, chunk_rows, heads, width,
    tile, step_hbm, rate_hbm, gain_hbm, hidden_hbm, weight_hbm, x_hbm, dy_hbm,
    grad_x, grad_step, out, rate_out, skip_out,
    step, log_rate, gain, hidden, weight, x, dy, spread_all, zs, tt, rt, back_all, dx, qt, g, l_row, l_col, r_row, t_col, w, small, acc, sacc, *rest
):
    bufs = rest[: len(plans)]
    sbuf, sems_send, sems_recv, sems_load = rest[len(plans) :]
    seq, dp = lax.axis_index("seq"), lax.axis_index("dp")
    first = seq == 0
    share = out.shape[0]
    tokens = x.shape[0]
    state = weight.shape[1] // 2
    slabs = x.shape[1] // SLAB

    def flipped(bit):
        mine = lax.rem(dp // (1 << bit), 2)
        return mine, dp + (1 - 2 * mine) * (1 << bit)

    other = 1 - seq
    loads = [
        pltpu.make_async_copy(src, dst, sems_load.at[n])
        for n, (src, dst) in enumerate((
            (step_hbm, step), (rate_hbm, log_rate), (gain_hbm, gain),
            (hidden_hbm, hidden), (weight_hbm, weight), (x_hbm, x), (dy_hbm, dy),
        ))
    ]
    for load in loads:
        load.start()
    barrier = pltpu.get_barrier_semaphore()
    pl.semaphore_signal(barrier, inc=1, device_id=(other, dp), device_id_type=MESH)
    for bit in range(bits):
        pl.semaphore_signal(barrier, inc=1, device_id=(seq, flipped(bit)[1]), device_id_type=MESH)

    count = [0]
    pending = []

    def send(src, dst, target):
        n = count[0]
        count[0] += 1
        copy = pltpu.make_async_remote_copy(
            src_ref=src, dst_ref=dst, send_sem=sems_send.at[n], recv_sem=sems_recv.at[n],
            device_id=target, device_id_type=MESH,
        )
        copy.start()
        pending.append(copy)
        return copy

    for n in range(slabs):
        spread_all[:, n * SLAB : (n + 1) * SLAB] = head_spread(n * SLAB, SLAB, width).astype(BF16)
    for load in loads[:3]:
        load.wait()
    mask = jnp.where(tile[0, 0] == 0, 1.0, 0.0).astype(F32)
    on_first = jnp.where(first, 1.0, 0.0).astype(F32)
    rate = -jnp.exp(to_column(log_rate[...], heads))
    masked = step[...] * mask
    rows = lax.broadcasted_iota(jnp.int32, (tokens, tokens), 0)
    cols = lax.broadcasted_iota(jnp.int32, (tokens, tokens), 1)
    running = dot(masked * rate, jnp.where(rows <= cols, 1.0, 0.0).astype(F32), precision=EXACT)
    alpha = jnp.where(first, jnp.exp(running[:, tokens - 1 :] - running) * masked, jnp.exp(running) * mask)
    alpha_high, alpha_low = split(pad_rows(alpha).T)
    both_alpha = jnp.concatenate([alpha_high, alpha_low], axis=1)
    gains = jnp.concatenate([gain[...] * mask, jnp.zeros((1, PAD - heads), F32)], axis=1)
    gain_parts = jnp.concatenate(split(jnp.broadcast_to(gains, (16, PAD))), axis=1)
    l_row[...] = running * LOG2E
    l_col[...] = pad_rows((running - jnp.log(step[...])) * LOG2E + (1.0 - mask) * 1e30).T

    loads[3].wait()
    loads[4].wait()
    projected = dot(hidden[...], weight[...])
    keys, query = projected[:, :state], projected[:, state:]
    both_keys = jnp.concatenate(split(jnp.where(first, keys, query)), axis=1)
    turned_keys = both_keys.T
    loads[5].wait()
    loads[6].wait()
    pl.semaphore_wait(barrier, bits + 1)
    swaps = []
    for n in range(slabs):
        at = slice(n * SLAB, (n + 1) * SLAB)
        spread = spread_all[:, at]
        wide = dot(both_alpha, jnp.concatenate([spread, spread], axis=0))
        z = jnp.where(first, x[:, at].astype(F32), dy[:, at].astype(F32))
        scaled, scaled_low = split(z * wide)
        zs[:, at] = scaled
        both = dot(turned_keys, scaled) + dot(turned_keys, scaled_low)
        tt[n] = both[:state] + both[state:]
        swaps.append(send(tt.at[n], rt.at[n], (other, dp)))

    heads_part(heads, width, x, dy, l_row, l_col, qt)
    key_parts = jnp.concatenate(split(keys), axis=1)
    query_parts = jnp.concatenate(split(query), axis=1)
    q_high, q_low = split(qt[...])
    grad_b = dot(q_high, query_parts) + dot(q_low, query_parts)
    grad_c = dot(q_high, key_parts, ((0,), (0,))) + dot(q_low, key_parts, ((0,), (0,)))
    grad_keys = jnp.zeros((tokens, 2 * state), F32)
    for n in range(slabs):
        swaps[n].wait_recv()
        at = slice(n * SLAB, (n + 1) * SLAB)
        grad_keys += dot(zs[:, at], jnp.concatenate(split(rt[n]), axis=0), ((1,), (1,)))
    grad_b += on_first * grad_keys
    grad_c += (1.0 - on_first) * grad_keys
    grad_p = jnp.concatenate(
        [grad_b[:, :state] + grad_b[:, state:], grad_c[:, :state] + grad_c[:, state:]], axis=1
    ).astype(BF16)

    def aligned(v):
        return pl.multiple_of(v, 8)

    def weight_rows(start, rows):
        w[pl.ds(aligned(start), rows), :] = dot(
            hidden[:, pl.ds(pl.multiple_of(start, PAD), rows)], grad_p, ((0,), (0,))
        )

    chunks = range(len(plans))
    bases = [sum(chunk_rows[:c]) for c in range(len(plans))]
    copies = [None] * len(plans)
    for c in chunks:
        size = chunk_rows[c]
        weight_rows(other * share + bases[c], size)
        copies[c] = send(
            w.at[pl.ds(aligned(other * share + bases[c]), size)], bufs[c].at[pl.ds(0, size)], (other, dp)
        )

    pair_args = (width, x, dy, l_row, g, dx, r_row, t_col)
    scale = 1.0 / scenes
    terms = {"carried": jnp.zeros((tokens, PAD), F32), "skip": jnp.zeros((8, PAD), F32)}
    light = [-1, None]

    def run_pairs(lo, hi):
        if lo == 0:
            g[...] = dot(keys, query, ((1,), (1,)), EXACT)
            t_col[...] = jnp.zeros_like(t_col)

        if hi - lo > 1:

            @pl.loop(0, (hi - lo) // 2)
            def _(n):
                turned = turn(l_col, lo + 2 * n)
                one_pair(lo + 2 * n, turned, 0, *pair_args)
                one_pair(lo + 2 * n + 1, turned, 2, *pair_args)

        if (hi - lo) % 2:
            one_pair(hi - 1, turn(l_col, hi - 1), 0, *pair_args)

    def run_carried(n):
        at = slice(n * SLAB, (n + 1) * SLAB)
        spread = spread_all[:, at]
        r_high, r_low = split(rt[n])
        back = dot(both_keys, jnp.concatenate([r_high, r_high], axis=0)) + dot(both_keys[:, :state], r_low)
        back_all[:, at] = back
        p_high, p_low = split(zs[:, at].astype(F32) * back)
        total = jnp.sum(x[:, at].astype(F32) * dy[:, at].astype(F32), axis=0, keepdims=True)
        t_high, t_low = split(jnp.broadcast_to(total, (16, SLAB)))
        summed = dot(jnp.concatenate([p_high, p_low, t_high, t_low], axis=0), spread, ((1,), (1,)))
        terms["carried"] += summed[:tokens] + summed[tokens : 2 * tokens]
        terms["skip"] += summed[2 * tokens : 2 * tokens + 8] + summed[2 * tokens + 16 : 2 * tokens + 24]

    def run_input(n):
        at = slice(n * SLAB, (n + 1) * SLAB)
        spread = spread_all[:, at]
        both = dot(
            jnp.concatenate([both_alpha, gain_parts], axis=0), jnp.concatenate([spread, spread], axis=0)
        )
        wide, gain_row = both[:tokens] * on_first, both[tokens : tokens + 1]
        grad_x[:, at] = (dx[:, at] + wide * back_all[:, at] + gain_row * dy[:, at].astype(F32)).astype(BF16)

    def run_last():
        crossing = terms["carried"].T[:heads]
        weighted = t_col[...].T[:heads]
        sign = 1.0 - 2.0 * on_first
        grad_l = r_row[...] - weighted + sign * crossing
        upper = jnp.where(rows >= cols, 1.0, 0.0).astype(F32)
        grad_log = dot(grad_l, upper, precision=EXACT)
        grad_log += on_first * jnp.sum(crossing, axis=1, keepdims=True)
        grad_step[...] = mask * ((weighted + on_first * crossing) / step[...] + rate * grad_log)
        grad_rate = jnp.sum(grad_log * masked, axis=1, keepdims=True) * rate
        row = lax.broadcasted_iota(jnp.int32, (8, PAD), 0)
        small[...] = jnp.where(row == 0, to_row(grad_rate, heads), jnp.where(row == 1, terms["skip"] * mask, 0.0))
        advance_small()

    def advance_small():
        stage = light[0]
        if stage > bits:
            return
        if stage >= 0:
            light[1].wait_recv()
            sacc[stage] = (small[...] if stage == 0 else sacc[stage - 1]) + sbuf[stage]
        light[0] = stage = stage + 1
        if stage == 0:
            light[1] = send(small, sbuf.at[0], (other, dp))
        elif stage <= bits:
            light[1] = send(sacc.at[stage - 1], sbuf.at[stage], (seq, flipped(stage - 1)[1]))

    quotas = list(QUOTAS)
    done = [0]
    pairs = heads // 2
    work = [functools.partial(run_carried, n) for n in range(slabs)] + [run_last]
    work += [functools.partial(run_input, n) for n in range(slabs)]

    def tick():
        n = quotas.pop(0) if quotas else 1
        if light[0] >= 0:
            advance_small()
        end = min(done[0] + n, pairs + len(work))
        if done[0] < min(end, pairs):
            run_pairs(done[0], min(end, pairs))
        for unit in range(max(done[0], pairs), end):
            work[unit - pairs]()
        done[0] = max(end, done[0])

    starts = list(bases)
    offsets = list(chunk_rows)
    history = [[] for _ in plans]

    def start_step(c, s):
        bit, kept, halves = plans[c][s]
        side, peer = flipped(bit)
        begin = starts[c]
        source = begin
        if halves:
            source = aligned(begin + (1 - side) * kept)
            starts[c] = aligned(begin + side * kept)
        offset = offsets[c]
        offsets[c] = offset + kept
        history[c].append((bit, kept, halves, starts[c]))
        copies[c] = send(acc.at[pl.ds(source, kept)], bufs[c].at[pl.ds(offset, kept)], (seq, peer))

    for c in chunks:
        weight_rows(seq * share + bases[c], chunk_rows[c])
    tick()
    for c in chunks:
        rows_here = chunk_rows[c]
        copies[c].wait_recv()
        mine = w[pl.ds(aligned(seq * share + bases[c]), rows_here), :]
        acc[pl.ds(bases[c], rows_here), :] = mine + bufs[c][0:rows_here, :]
        start_step(c, 0)

    for s in range(bits):
        for c in chunks:
            tick()
            kept, halves = plans[c][s][1:]
            copies[c].wait_recv()
            if not halves:
                copies[c].wait_send()
                pending[:] = [p for p in pending if p is not copies[c]]
            here = pl.ds(starts[c], kept)
            acc[here, :] = acc[here, :] + bufs[c][offsets[c] - kept : offsets[c], :]
            if s + 1 < bits:
                start_step(c, s + 1)
            else:
                out[here, :] = acc[here, :] * scale

    trail = [[h for h in reversed(history[c]) if h[2]] for c in range(len(plans))]

    def gather(c, n):
        bit, kept, _, start = trail[c][n]
        region = out.at[pl.ds(start, kept)]
        return send(region, region, (seq, flipped(bit)[1]))

    for c in chunks:
        copies[c] = gather(c, 0)
    for n in range(max(len(t) for t in trail)):
        for c in chunks:
            if n < len(trail[c]):
                tick()
                copies[c].wait_recv()
                if n + 1 < len(trail[c]):
                    copies[c] = gather(c, n + 1)
    while light[0] <= bits or done[0] < pairs + len(work):
        tick()
    total = sacc[bits] * scale
    total = jnp.where(seq == 0, total, pltpu.roll(total, PAD - heads // 2, 1))
    rate_out[...] = total[0:1, : heads // 2]
    skip_out[...] = total[1:2, : heads // 2]
    for copy in pending:
        copy.wait_send()


def chunk_orders(bits):
    if bits < 4:
        return [list(range(bits))] * 3
    late = list(range(3, bits))
    return [0, 2, 1] + late, [1, 0, 2] + late, [2, 1, 0] + late


def shards(hidden, scan_input, grad_out, step_size, proj_weight, log_rate, skip_gain, tile_list):
    tokens, inner = scan_input.shape[1:]
    model, two_state = proj_weight.shape
    heads = log_rate.shape[0]
    width = inner // heads
    slabs, state = inner // SLAB, two_state // 2
    scenes, seqs = lax.axis_size("dp"), lax.axis_size("seq")
    bits = scenes.bit_length() - 1
    rows = model // seqs
    low = rows // (3 * PAD) * PAD
    chunk_rows = (low, low, rows - 2 * low)
    plans = [plan(r, bits, o) for r, o in zip(chunk_rows, chunk_orders(bits))]

    def shape(*dims, dtype=F32):
        return jax.ShapeDtypeStruct(dims, dtype)

    scratch = [
        pltpu.VMEM((heads, tokens), F32), pltpu.VMEM((1, heads), F32), pltpu.VMEM((1, heads), F32),
        pltpu.VMEM((tokens, model), BF16), pltpu.VMEM((model, two_state), BF16),
        pltpu.VMEM((tokens, inner), BF16), pltpu.VMEM((tokens, inner), BF16),
        pltpu.VMEM((PAD, inner), BF16), pltpu.VMEM((tokens, inner), BF16),
        pltpu.VMEM((slabs, state, SLAB), F32), pltpu.VMEM((slabs, state, SLAB), F32),
        pltpu.VMEM((tokens, inner), F32), pltpu.VMEM((tokens, inner), F32),
        pltpu.VMEM((tokens, tokens), F32), pltpu.VMEM((tokens, tokens), F32),
        pltpu.VMEM((heads, tokens), F32), pltpu.VMEM((tokens, PAD), F32),
        pltpu.VMEM((heads, tokens), F32), pltpu.VMEM((tokens, PAD), F32),
        pltpu.VMEM((model, two_state), F32), pltpu.VMEM((8, PAD), F32),
        pltpu.VMEM((rows, two_state), F32), pltpu.VMEM((bits + 1, 8, PAD), F32),
    ]
    for r, steps in zip(chunk_rows, plans):
        scratch.append(pltpu.VMEM((r + sum(k for _, k, _ in steps), two_state), F32))
    scratch.append(pltpu.VMEM((bits + 1, 8, PAD), F32))
    copies = slabs + len(plans) * (1 + 2 * bits) + bits + 1
    scratch += [pltpu.SemaphoreType.DMA((copies,)), pltpu.SemaphoreType.DMA((copies,)), pltpu.SemaphoreType.DMA((7,))]
    stored = pl.BlockSpec(memory_space=pltpu.HBM)
    out_shape = (
        shape(tokens, inner, dtype=BF16), shape(heads, tokens), shape(rows, two_state),
        shape(1, heads // seqs), shape(1, heads // seqs),
    )
    grad_x, grad_step, summed, rates, gains = pl.pallas_call(
        functools.partial(layer_kernel, bits, scenes, plans, chunk_rows, heads, width),
        out_shape=out_shape,
        in_specs=[SMEM] + [stored] * 7,
        out_specs=(VMEM,) * 5,
        scratch_shapes=scratch,
        compiler_params=pltpu.CompilerParams(
            collective_id=0, has_side_effects=True, vmem_limit_bytes=60 * 1024 * 1024
        ),
        name="layer",
    )(
        tile_list, step_size[0], log_rate[None], skip_gain[None],
        hidden[0], proj_weight, scan_input[0], grad_out[0],
    )
    return grad_x[None], grad_step[None], summed, rates[0], gains[0]


def solution(mesh):
    in_specs = (
        P("dp", "seq", None),
        P("dp", "seq", None),
        P("dp", "seq", None),
        P("dp", None, "seq"),
        P(),
        P(),
        P(),
        P("dp", "seq"),
    )
    out_specs = (P("dp", "seq", None), P("dp", None, "seq"), P("seq", None), P("seq"), P("seq"))
    return jax.shard_map(shards, mesh=mesh, in_specs=in_specs, out_specs=out_specs, check_vma=False)
```

```python
import functools

import jax
import jax.numpy as jnp
from jax import lax
from jax.experimental import pallas as pl
from jax.experimental.pallas import tpu as pltpu
from jax.sharding import PartitionSpec as P

MESH = pl.DeviceIdType.MESH
EXACT = lax.Precision.HIGHEST
F32 = jnp.float32
BF16 = jnp.bfloat16
LOG2E = 1.4426950408889634
PAD = 128
SLAB = 512
QUOTAS = (2, 6, 0, 0, 4, 0, 0, 2, 2, 0, 4, 1, 0, 2, 1, 0, 1, 1, 0, 1, 1, 0, 1, 1, 1)
VMEM = pl.BlockSpec(memory_space=pltpu.VMEM)
SMEM = pl.BlockSpec(memory_space=pltpu.SMEM)


def dot(a, b, dims=((1,), (0,)), precision=None):
    return lax.dot_general(a, b, (dims, ((), ())), precision=precision, preferred_element_type=F32)


def split(a):
    high = a.astype(BF16)
    return high, (a - high.astype(F32)).astype(BF16)


def to_column(row, count):
    rows = lax.broadcasted_iota(jnp.int32, (count, count), 0)
    cols = lax.broadcasted_iota(jnp.int32, (count, count), 1)
    return jnp.sum(jnp.where(rows == cols, row, 0.0), axis=1, keepdims=True)


def to_row(column, count):
    rows = lax.broadcasted_iota(jnp.int32, (count, PAD), 0)
    cols = lax.broadcasted_iota(jnp.int32, (count, PAD), 1)
    return jnp.sum(jnp.where(rows == cols, column, 0.0), axis=0, keepdims=True)


def head_spread(start, size, width):
    rows = lax.broadcasted_iota(jnp.int32, (PAD, size), 0)
    cols = lax.broadcasted_iota(jnp.int32, (PAD, size), 1) + start
    return jnp.where((cols >= rows * width) & (cols < (rows + 1) * width), 1.0, 0.0).astype(F32)


def pad_rows(a):
    return jnp.concatenate([a, jnp.zeros((PAD - a.shape[0], a.shape[1]), a.dtype)], axis=0)


def pair_parts(k, turned, lane, width, x, dy, l_row):
    tokens = x.shape[0]
    half = tokens // 2
    pair = 2 * width
    rows = lax.broadcasted_iota(jnp.int32, (half, half), 0)
    cols = lax.broadcasted_iota(jnp.int32, (half, half), 1)
    causal = cols >= rows
    in_first = lax.broadcasted_iota(jnp.int32, (1, pair), 1) < width
    keep = [jnp.where(in_first, 1.0, 0.0).astype(BF16), jnp.where(in_first, 0.0, 1.0).astype(BF16)]
    at = pl.ds(pl.multiple_of(k * pair, pair), pair)
    x2 = x[:, at]
    dy2 = dy[:, at]
    sides = []
    for side in range(2):
        l_j = turned[:, lane + side : lane + side + 1]
        l_i = l_row[pl.ds(2 * k + side, 1), :]
        xs = x2 * keep[side]
        w_top = dot(xs[:half], dy2, ((1,), (1,)))
        w_low = dot(xs[half:], dy2[half:], ((1,), (1,)))
        d00 = jnp.exp2(jnp.where(causal, l_i[:, :half] - l_j[:half], -1e30))
        d01 = jnp.exp2(l_i[:, half:] - l_j[:half])
        d11 = jnp.exp2(jnp.where(causal, l_i[:, half:] - l_j[half:], -1e30))
        sides.append(((d00, w_top[:, :half]), (d01, w_top[:, half:]), (d11, w_low)))
    return at, dy2, in_first, sides


def turn(l_col, k):
    return pltpu.roll(l_col[...], lax.rem(PAD - 2 * k, PAD), 1)


def heads_part(heads, width, x, dy, l_row, l_col, qt):
    half = x.shape[0] // 2
    qt[...] = jnp.zeros_like(qt)
    group = 4 if heads % 8 == 0 else 1

    @pl.loop(0, heads // 2 // group)
    def _(step):
        turned = turn(l_col, step * group)
        parts = []
        for n in range(group):
            parts += pair_parts(step * group + n, turned, 2 * n, width, x, dy, l_row)[3]
        for n, (j, i) in enumerate(((0, 0), (0, 1), (1, 1))):
            js, at_i = slice(j * half, (j + 1) * half), slice(i * half, (i + 1) * half)
            qt[js, at_i] += sum(side[n][0] * side[n][1] for side in parts)


def one_pair(k, turned, lane, width, x, dy, l_row, g, dx, r_row, t_col):
    tokens = x.shape[0]
    half = tokens // 2
    lanes = lax.broadcasted_iota(jnp.int32, (tokens, PAD), 1)
    at, dy2, in_first, sides = pair_parts(k, turned, lane, width, x, dy, l_row)
    sums = t_col[...]
    pieces = []
    for side in range(2):
        head = 2 * k + side
        (d00, w00), (d01, w01), (d11, w11) = sides[side]
        m00, m01, m11 = d00 * g[:half, :half], d01 * g[:half, half:], d11 * g[half:, half:]
        e00, e01, e11 = m00 * w00, m01 * w01, m11 * w11
        r_row[pl.ds(head, 1), :] = jnp.concatenate(
            [jnp.sum(e00, axis=0, keepdims=True), jnp.sum(e01 + e11, axis=0, keepdims=True)], axis=1
        )
        column = jnp.concatenate(
            [jnp.sum(e00 + e01, axis=1, keepdims=True), jnp.sum(e11, axis=1, keepdims=True)], axis=0
        )
        sums = jnp.where(lanes == head, column, sums)
        top_high, top_low = split(jnp.concatenate([m00, m01], axis=1))
        low_high, low_low = split(m11)
        top = dot(top_high, dy2) + dot(top_low, dy2)
        low = dot(low_high, dy2[half:]) + dot(low_low, dy2[half:])
        pieces.append((top, low))
    t_col[...] = sums
    dx[:half, at] = jnp.where(in_first, pieces[0][0], pieces[1][0])
    dx[half:, at] = jnp.where(in_first, pieces[0][1], pieces[1][1])


def plan(rows, bits, order):
    steps = []
    for bit in order:
        halves = rows % 16 == 0
        rows = rows // 2 if halves else rows
        steps.append((bit, rows, halves))
    return steps


def layer_kernel(
    bits, scenes, plans, chunk_rows, heads, width,
    tile, step_hbm, rate_hbm, gain_hbm, hidden_hbm, weight_hbm, x_hbm, dy_hbm,
    grad_x, grad_step, out, rate_out, skip_out,
    step, log_rate, gain, hidden, weight, x, dy, spread_all, zs, tt, rt, back_all, dx, qt, g, l_row, l_col, r_row, t_col, w, small, acc, sacc, *rest
):
    bufs = rest[: len(plans)]
    sbuf, sems_send, sems_recv, sems_load = rest[len(plans) :]
    seq, dp = lax.axis_index("seq"), lax.axis_index("dp")
    first = seq == 0
    share = out.shape[0]
    tokens = x.shape[0]
    state = weight.shape[1] // 2
    slabs = x.shape[1] // SLAB

    def flipped(bit):
        mine = lax.rem(dp // (1 << bit), 2)
        return mine, dp + (1 - 2 * mine) * (1 << bit)

    other = 1 - seq
    loads = [
        pltpu.make_async_copy(src, dst, sems_load.at[n])
        for n, (src, dst) in enumerate((
            (step_hbm, step), (rate_hbm, log_rate), (gain_hbm, gain),
            (hidden_hbm, hidden), (weight_hbm, weight), (x_hbm, x), (dy_hbm, dy),
        ))
    ]
    for load in loads:
        load.start()
    barrier = pltpu.get_barrier_semaphore()
    pl.semaphore_signal(barrier, inc=1, device_id=(other, dp), device_id_type=MESH)
    for bit in range(bits):
        pl.semaphore_signal(barrier, inc=1, device_id=(seq, flipped(bit)[1]), device_id_type=MESH)

    count = [0]
    pending = []

    def send(src, dst, target):
        n = count[0]
        count[0] += 1
        copy = pltpu.make_async_remote_copy(
            src_ref=src, dst_ref=dst, send_sem=sems_send.at[n], recv_sem=sems_recv.at[n],
            device_id=target, device_id_type=MESH,
        )
        copy.start()
        pending.append(copy)
        return copy

    for n in range(slabs):
        spread_all[:, n * SLAB : (n + 1) * SLAB] = head_spread(n * SLAB, SLAB, width).astype(BF16)
    for load in loads[:3]:
        load.wait()
    mask = jnp.where(tile[0, 0] == 0, 1.0, 0.0).astype(F32)
    on_first = jnp.where(first, 1.0, 0.0).astype(F32)
    rate = -jnp.exp(to_column(log_rate[...], heads))
    masked = step[...] * mask
    rows = lax.broadcasted_iota(jnp.int32, (tokens, tokens), 0)
    cols = lax.broadcasted_iota(jnp.int32, (tokens, tokens), 1)
    running = dot(masked * rate, jnp.where(rows <= cols, 1.0, 0.0).astype(F32), precision=EXACT)
    alpha = jnp.where(first, jnp.exp(running[:, tokens - 1 :] - running) * masked, jnp.exp(running) * mask)
    alpha_high, alpha_low = split(pad_rows(alpha).T)
    both_alpha = jnp.concatenate([alpha_high, alpha_low], axis=1)
    gains = jnp.concatenate([gain[...] * mask, jnp.zeros((1, PAD - heads), F32)], axis=1)
    gain_parts = jnp.concatenate(split(jnp.broadcast_to(gains, (16, PAD))), axis=1)
    l_row[...] = running * LOG2E
    l_col[...] = pad_rows((running - jnp.log(step[...])) * LOG2E + (1.0 - mask) * 1e30).T

    loads[3].wait()
    loads[4].wait()
    projected = dot(hidden[...], weight[...])
    keys, query = projected[:, :state], projected[:, state:]
    both_keys = jnp.concatenate(split(jnp.where(first, keys, query)), axis=1)
    turned_keys = both_keys.T
    loads[5].wait()
    loads[6].wait()
    pl.semaphore_wait(barrier, bits + 1)
    swaps = []
    for n in range(slabs):
        at = slice(n * SLAB, (n + 1) * SLAB)
        spread = spread_all[:, at]
        wide = dot(both_alpha, jnp.concatenate([spread, spread], axis=0))
        z = jnp.where(first, x[:, at].astype(F32), dy[:, at].astype(F32))
        scaled, scaled_low = split(z * wide)
        zs[:, at] = scaled
        both = dot(turned_keys, scaled) + dot(turned_keys, scaled_low)
        tt[n] = both[:state] + both[state:]
        swaps.append(send(tt.at[n], rt.at[n], (other, dp)))

    heads_part(heads, width, x, dy, l_row, l_col, qt)
    key_parts = jnp.concatenate(split(keys), axis=1)
    query_parts = jnp.concatenate(split(query), axis=1)
    q_high, q_low = split(qt[...])
    grad_b = dot(q_high, query_parts) + dot(q_low, query_parts)
    grad_c = dot(q_high, key_parts, ((0,), (0,))) + dot(q_low, key_parts, ((0,), (0,)))
    grad_keys = jnp.zeros((tokens, 2 * state), F32)
    for n in range(slabs):
        swaps[n].wait_recv()
        at = slice(n * SLAB, (n + 1) * SLAB)
        grad_keys += dot(zs[:, at], jnp.concatenate(split(rt[n]), axis=0), ((1,), (1,)))
    grad_b += on_first * grad_keys
    grad_c += (1.0 - on_first) * grad_keys
    grad_p = jnp.concatenate(
        [grad_b[:, :state] + grad_b[:, state:], grad_c[:, :state] + grad_c[:, state:]], axis=1
    ).astype(BF16)

    def aligned(v):
        return pl.multiple_of(v, 8)

    def weight_rows(start, rows):
        w[pl.ds(aligned(start), rows), :] = dot(
            hidden[:, pl.ds(pl.multiple_of(start, PAD), rows)], grad_p, ((0,), (0,))
        )

    chunks = range(len(plans))
    bases = [sum(chunk_rows[:c]) for c in range(len(plans))]
    copies = [None] * len(plans)
    for c in chunks:
        size = chunk_rows[c]
        weight_rows(other * share + bases[c], size)
        copies[c] = send(
            w.at[pl.ds(aligned(other * share + bases[c]), size)], bufs[c].at[pl.ds(0, size)], (other, dp)
        )

    pair_args = (width, x, dy, l_row, g, dx, r_row, t_col)
    scale = 1.0 / scenes
    terms = {"carried": jnp.zeros((tokens, PAD), F32), "skip": jnp.zeros((8, PAD), F32)}
    light = [-1, None]

    def run_pairs(lo, hi):
        if lo == 0:
            g[...] = dot(keys, query, ((1,), (1,)), EXACT)
            t_col[...] = jnp.zeros_like(t_col)

        if hi - lo > 1:

            @pl.loop(0, (hi - lo) // 2)
            def _(n):
                turned = turn(l_col, lo + 2 * n)
                one_pair(lo + 2 * n, turned, 0, *pair_args)
                one_pair(lo + 2 * n + 1, turned, 2, *pair_args)

        if (hi - lo) % 2:
            one_pair(hi - 1, turn(l_col, hi - 1), 0, *pair_args)

    def run_carried(n):
        at = slice(n * SLAB, (n + 1) * SLAB)
        spread = spread_all[:, at]
        r_high, r_low = split(rt[n])
        back = dot(both_keys, jnp.concatenate([r_high, r_high], axis=0)) + dot(both_keys[:, :state], r_low)
        back_all[:, at] = back
        p_high, p_low = split(zs[:, at].astype(F32) * back)
        total = jnp.sum(x[:, at].astype(F32) * dy[:, at].astype(F32), axis=0, keepdims=True)
        t_high, t_low = split(jnp.broadcast_to(total, (16, SLAB)))
        summed = dot(jnp.concatenate([p_high, p_low, t_high, t_low], axis=0), spread, ((1,), (1,)))
        terms["carried"] += summed[:tokens] + summed[tokens : 2 * tokens]
        terms["skip"] += summed[2 * tokens : 2 * tokens + 8] + summed[2 * tokens + 16 : 2 * tokens + 24]

    def run_input(n):
        at = slice(n * SLAB, (n + 1) * SLAB)
        spread = spread_all[:, at]
        both = dot(
            jnp.concatenate([both_alpha, gain_parts], axis=0), jnp.concatenate([spread, spread], axis=0)
        )
        wide, gain_row = both[:tokens] * on_first, both[tokens : tokens + 1]
        grad_x[:, at] = (dx[:, at] + wide * back_all[:, at] + gain_row * dy[:, at].astype(F32)).astype(BF16)

    def run_last():
        crossing = terms["carried"].T[:heads]
        weighted = t_col[...].T[:heads]
        sign = 1.0 - 2.0 * on_first
        grad_l = r_row[...] - weighted + sign * crossing
        upper = jnp.where(rows >= cols, 1.0, 0.0).astype(F32)
        grad_log = dot(grad_l, upper, precision=EXACT)
        grad_log += on_first * jnp.sum(crossing, axis=1, keepdims=True)
        grad_step[...] = mask * ((weighted + on_first * crossing) / step[...] + rate * grad_log)
        grad_rate = jnp.sum(grad_log * masked, axis=1, keepdims=True) * rate
        row = lax.broadcasted_iota(jnp.int32, (8, PAD), 0)
        small[...] = jnp.where(row == 0, to_row(grad_rate, heads), jnp.where(row == 1, terms["skip"] * mask, 0.0))
        advance_small()

    def advance_small():
        stage = light[0]
        if stage > bits:
            return
        if stage >= 0:
            light[1].wait_recv()
            sacc[stage] = (small[...] if stage == 0 else sacc[stage - 1]) + sbuf[stage]
        light[0] = stage = stage + 1
        if stage == 0:
            light[1] = send(small, sbuf.at[0], (other, dp))
        elif stage <= bits:
            light[1] = send(sacc.at[stage - 1], sbuf.at[stage], (seq, flipped(stage - 1)[1]))

    quotas = list(QUOTAS)
    done = [0]
    pairs = heads // 2
    work = [functools.partial(run_carried, n) for n in range(slabs)] + [run_last]
    work += [functools.partial(run_input, n) for n in range(slabs)]

    def tick():
        n = quotas.pop(0) if quotas else 1
        if light[0] >= 0:
            advance_small()
        end = min(done[0] + n, pairs + len(work))
        if done[0] < min(end, pairs):
            run_pairs(done[0], min(end, pairs))
        for unit in range(max(done[0], pairs), end):
            work[unit - pairs]()
        done[0] = max(end, done[0])

    starts = list(bases)
    offsets = list(chunk_rows)
    history = [[] for _ in plans]

    def start_step(c, s):
        bit, kept, halves = plans[c][s]
        side, peer = flipped(bit)
        begin = starts[c]
        source = begin
        if halves:
            source = aligned(begin + (1 - side) * kept)
            starts[c] = aligned(begin + side * kept)
        offset = offsets[c]
        offsets[c] = offset + kept
        history[c].append((bit, kept, halves, starts[c]))
        copies[c] = send(acc.at[pl.ds(source, kept)], bufs[c].at[pl.ds(offset, kept)], (seq, peer))

    for c in chunks:
        weight_rows(seq * share + bases[c], chunk_rows[c])
    tick()
    for c in chunks:
        rows_here = chunk_rows[c]
        copies[c].wait_recv()
        mine = w[pl.ds(aligned(seq * share + bases[c]), rows_here), :]
        acc[pl.ds(bases[c], rows_here), :] = mine + bufs[c][0:rows_here, :]
        start_step(c, 0)

    for s in range(bits):
        for c in chunks:
            tick()
            kept, halves = plans[c][s][1:]
            copies[c].wait_recv()
            if not halves:
                copies[c].wait_send()
                pending[:] = [p for p in pending if p is not copies[c]]
            here = pl.ds(starts[c], kept)
            acc[here, :] = acc[here, :] + bufs[c][offsets[c] - kept : offsets[c], :]
            if s + 1 < bits:
                start_step(c, s + 1)
            else:
                out[here, :] = acc[here, :] * scale

    trail = [[h for h in reversed(history[c]) if h[2]] for c in range(len(plans))]

    def gather(c, n):
        bit, kept, _, start = trail[c][n]
        region = out.at[pl.ds(start, kept)]
        return send(region, region, (seq, flipped(bit)[1]))

    for c in chunks:
        copies[c] = gather(c, 0)
    for n in range(max(len(t) for t in trail)):
        for c in chunks:
            if n < len(trail[c]):
                tick()
                copies[c].wait_recv()
                if n + 1 < len(trail[c]):
                    copies[c] = gather(c, n + 1)
    while light[0] <= bits or done[0] < pairs + len(work):
        tick()
    total = sacc[bits] * scale
    total = jnp.where(seq == 0, total, pltpu.roll(total, PAD - heads // 2, 1))
    rate_out[...] = total[0:1, : heads // 2]
    skip_out[...] = total[1:2, : heads // 2]
    for copy in pending:
        copy.wait_send()


def chunk_orders(bits):
    if bits < 4:
        return [list(range(bits))] * 3
    late = list(range(3, bits))
    return [0, 2, 1] + late, [1, 0, 2] + late, [2, 1, 0] + late


def shards(hidden, scan_input, grad_out, step_size, proj_weight, log_rate, skip_gain, tile_list):
    tokens, inner = scan_input.shape[1:]
    model, two_state = proj_weight.shape
    heads = log_rate.shape[0]
    width = inner // heads
    slabs, state = inner // SLAB, two_state // 2
    scenes, seqs = lax.axis_size("dp"), lax.axis_size("seq")
    bits = scenes.bit_length() - 1
    rows = model // seqs
    low = rows // (3 * PAD) * PAD
    chunk_rows = (low, low, rows - 2 * low)
    plans = [plan(r, bits, o) for r, o in zip(chunk_rows, chunk_orders(bits))]

    def shape(*dims, dtype=F32):
        return jax.ShapeDtypeStruct(dims, dtype)

    scratch = [
        pltpu.VMEM((heads, tokens), F32), pltpu.VMEM((1, heads), F32), pltpu.VMEM((1, heads), F32),
        pltpu.VMEM((tokens, model), BF16), pltpu.VMEM((model, two_state), BF16),
        pltpu.VMEM((tokens, inner), BF16), pltpu.VMEM((tokens, inner), BF16),
        pltpu.VMEM((PAD, inner), BF16), pltpu.VMEM((tokens, inner), BF16),
        pltpu.VMEM((slabs, state, SLAB), F32), pltpu.VMEM((slabs, state, SLAB), F32),
        pltpu.VMEM((tokens, inner), F32), pltpu.VMEM((tokens, inner), F32),
        pltpu.VMEM((tokens, tokens), F32), pltpu.VMEM((tokens, tokens), F32),
        pltpu.VMEM((heads, tokens), F32), pltpu.VMEM((tokens, PAD), F32),
        pltpu.VMEM((heads, tokens), F32), pltpu.VMEM((tokens, PAD), F32),
        pltpu.VMEM((model, two_state), F32), pltpu.VMEM((8, PAD), F32),
        pltpu.VMEM((rows, two_state), F32), pltpu.VMEM((bits + 1, 8, PAD), F32),
    ]
    for r, steps in zip(chunk_rows, plans):
        scratch.append(pltpu.VMEM((r + sum(k for _, k, _ in steps), two_state), F32))
    scratch.append(pltpu.VMEM((bits + 1, 8, PAD), F32))
    copies = slabs + len(plans) * (1 + 2 * bits) + bits + 1
    scratch += [pltpu.SemaphoreType.DMA((copies,)), pltpu.SemaphoreType.DMA((copies,)), pltpu.SemaphoreType.DMA((7,))]
    stored = pl.BlockSpec(memory_space=pltpu.HBM)
    out_shape = (
        shape(tokens, inner, dtype=BF16), shape(heads, tokens), shape(rows, two_state),
        shape(1, heads // seqs), shape(1, heads // seqs),
    )
    grad_x, grad_step, summed, rates, gains = pl.pallas_call(
        functools.partial(layer_kernel, bits, scenes, plans, chunk_rows, heads, width),
        out_shape=out_shape,
        in_specs=[SMEM] + [stored] * 7,
        out_specs=(VMEM,) * 5,
        scratch_shapes=scratch,
        compiler_params=pltpu.CompilerParams(
            collective_id=0, has_side_effects=True, vmem_limit_bytes=58 * 1024 * 1024
        ),
        name="layer",
    )(
        tile_list, step_size[0], log_rate[None], skip_gain[None],
        hidden[0], proj_weight, scan_input[0], grad_out[0],
    )
    return grad_x[None], grad_step[None], summed, rates[0], gains[0]


def solution(mesh):
    in_specs = (
        P("dp", "seq", None),
        P("dp", "seq", None),
        P("dp", "seq", None),
        P("dp", None, "seq"),
        P(),
        P(),
        P(),
        P("dp", "seq"),
    )
    out_specs = (P("dp", "seq", None), P("dp", None, "seq"), P("seq", None), P("seq"), P("seq"))
    return jax.shard_map(shards, mesh=mesh, in_specs=in_specs, out_specs=out_specs, check_vma=False)
```
